256 devices in a mesh: phase: 2 (over core), batch: 8 (over z), seq: 16 (over y, x).
Axes of the slice: x: 4, y: 4, z: 8, core: 2. Of those that a mesh axis runs over, the one named last changes fastest.
Arguments:
- features: bfloat16 [8, 8192, 128], P('batch', 'seq'), may hold values from -6 to 6
- lengths: int32 [8, 12], P('batch'), may hold values from 1 to 256, 2048 in all within a row
- conv1_weight: float32 [3, 3, 256], replicated, may hold values from -2 to 2
- conv1_bias: float32 [256], replicated, may hold values from -3 to 3
- conv2_weight: bfloat16 [3, 3, 256, 256], P(None, None, None, 'phase'), may hold values from -0.125 to 0.125
- conv2_bias: float32 [256], P('phase'), may hold values from -3 to 3
- proj_weight: bfloat16 [8192, 1536], P(('phase', 'seq')), may hold values from -0.0625 to 0.0625
- proj_bias: float32 [1536], replicated, may hold values from -6 to 6
- norm_gain: float32 [1536], replicated, may hold values from 0.25 to 1.75
- qkv_weight: bfloat16 [1536, 3, 1536], P(None, None, 'phase'), may hold values from -1 to 1
- out_weight: bfloat16 [1536, 1536], P('phase'), may hold values from -0.15625 to 0.15625
Outputs:
- encoded: bfloat16 [8, 2048, 1536], P('batch', 'seq', 'phase')
The draws below stay inside these ranges and needn't reach their ends.
Inputs may be any that keep to these rules, and one draw needn't show every extreme that they name: In each group the 12 lengths add up to 2048 and the largest is exactly 256; an utterance covers four times its length of input frames.
All inputs are finite; a program needn't handle non-finite values.
Results may differ from the reference program's by a relative error of at most 0.017.
Values may be sent and summed in bfloat16 or wider, within the bound.
A program may use at most 128 MiB of HBM per device.

```python
import math
import jax
import jax.numpy as jnp
import numpy as np
from jax import lax

D = 1536
HEAD = 64
CH = 256
MEL = 128
GROUPS = 8
GROUP_FRAMES = 2048
MOST = 256
UTTS = 12
PROJ_IN = 8192


def draw_proj_bias(key, part):
    return 0.5 * jnp.clip(jax.random.normal(jax.random.fold_in(key, 7002), (D,), jnp.float32), -6.0, 6.0)


def draw_qkv_weight(key, part):
    base = jnp.clip(jax.random.normal(jax.random.fold_in(key, 7003), (D, 3, D), jnp.float32), -6.0, 6.0) / math.sqrt(D)
    return jnp.clip(base, -1.0, 1.0).astype(jnp.bfloat16)


def block_levels(own_key, shape, split, smallest, top_value):
    loudness, own = 1.0, jax.random.fold_in(own_key, 6)
    for position, blocks in split:
        heights = jnp.exp(jax.random.uniform(jax.random.fold_in(own, position), (blocks,), jnp.float32, smallest / len(split), top_value / len(split)))
        loudness = loudness * jnp.repeat(heights, shape[position] // blocks).reshape([-1 if axis == position else 1 for axis in range(len(shape))])
    return loudness


def length_profile(amount, total, limit, slope):
    weights = [(1 << 20) // math.isqrt(grade ** slope) + 1 for grade in range(2, amount + 1)]
    spare, holding = total - limit - (amount - 1), [1] * (amount - 1)
    while spare > 0:
        movable = [i for i in range(amount - 1) if holding[i] < limit]
        pool, remaining = sum([weights[i] for i in movable]), spare
        for i in movable:
            addition = min(limit - holding[i], max(1, remaining * weights[i] // pool), spare)
            holding[i] = holding[i] + addition
            spare = spare - addition
    return np.array([limit] + holding)


def uneven_parts(stream_key, number_of, total, limit, lean):
    if number_of == 2:
        one = jax.random.randint(stream_key, (), max(1, total - limit), min(limit, total - 1) + 1)
        return jnp.stack([one, total - one])
    tallies = jnp.asarray(length_profile(number_of, total, limit, lean), jnp.int32)
    pairs = (number_of - 1) // 2
    donor, sink = tallies[1:1 + 2 * pairs:2], tallies[2:2 + 2 * pairs:2]
    slack = jnp.minimum(donor - 1, limit - sink)
    shifted = jax.random.randint(jax.random.fold_in(stream_key, 1), (pairs,), 0, 1 << 20) % (slack + 1)
    tallies = tallies.at[1:1 + 2 * pairs:2].set(donor - shifted).at[2:2 + 2 * pairs:2].set(sink + shifted)
    return tallies[jax.random.permutation(jax.random.fold_in(stream_key, 2), number_of)]


def scatter_about(key, shape, deviation, limit, split=(), held_as=jnp.bfloat16):
    loudness = block_levels(key, shape, split, -0.22, 0.18) if split else 1.0
    entries = jax.random.normal(key, shape, jnp.float32) * deviation * loudness
    return jnp.minimum(jnp.maximum(entries, -limit), limit).astype(held_as)


def setup_inputs(seed: int = 0) -> dict:
    streams_of = jax.random.split(jax.random.key(seed), 12)
    return {
        "features": scatter_about(streams_of[0], (GROUPS, 4 * GROUP_FRAMES, MEL), 1.0, 6.0, ((0, 8), (1, 16))),
        "lengths": jax.vmap(lambda own: uneven_parts(own, UTTS, GROUP_FRAMES, MOST, 2))(jax.random.split(streams_of[1], GROUPS)).reshape((GROUPS, UTTS)).astype(jnp.int32),
        "conv1_weight": scatter_about(streams_of[2], (3, 3, CH), 9 ** -0.5, 2.0, (), jnp.float32),
        "conv1_bias": scatter_about(streams_of[3], (CH,), 0.5, 3.0, (), jnp.float32),
        "conv2_weight": scatter_about(streams_of[4], (3, 3, CH, CH), (9 * CH) ** -0.5, 0.125, ((3, 2),)),
        "conv2_bias": scatter_about(streams_of[5], (CH,), 0.5, 3.0, ((0, 2),), jnp.float32),
        "proj_weight": scatter_about(streams_of[6], (PROJ_IN, D), PROJ_IN ** -0.5, 0.0625, ((0, 32),)),
        "proj_bias": draw_proj_bias(jax.random.fold_in(streams_of[11], 71), 0),
        "norm_gain": jnp.clip(1.0 + 0.15 * jax.random.normal(streams_of[8], (D,), jnp.float32), 0.25, 1.75),
        "qkv_weight": draw_qkv_weight(jax.random.fold_in(streams_of[11], 71), 0),
        "out_weight": scatter_about(streams_of[10], (D, D), D ** -0.5, 0.15625, ((0, 2),)),
    }


def segment_info(lengths_row, positions, group_len):
    offsets = jnp.cumsum(lengths_row, dtype=jnp.int32) - lengths_row
    starts = jnp.any(positions[:, None] == offsets[None, :], axis=1)
    inside = (positions >= 0) & (positions < group_len)
    counted = lax.optimization_barrier(jnp.sum((positions[:, None] >= offsets[None, :]).astype(jnp.int32), axis=1)) - 1
    return (starts, jnp.where(inside, counted, -1))

def first_conv(widened, kept, weights, biases):
    rows_out = (widened.shape[0] - 3) // 2 + 1
    bins = widened.shape[1]
    padded = jnp.pad(widened, ((0, 0), (1, 1)))
    ones_row = jnp.ones_like(kept)
    row_mask = jnp.concatenate([jnp.ones((1,), jnp.float32), jnp.stack([kept, ones_row], axis=1).reshape(-1)])
    summed = jnp.zeros((rows_out, bins // 2, weights.shape[2]), jnp.float32) + biases
    for step_time in range(3):
        for step_bin in range(3):
            tapped = padded[step_time:step_time + 2 * rows_out - 1:2, step_bin:step_bin + bins - 1:2]
            if step_time == 0:
                tapped = tapped * row_mask[:, None]
            summed = summed + tapped[:, :, None] * weights[step_time, step_bin]
    return jax.nn.relu(summed).astype(jnp.bfloat16)

def second_conv(first_maps, kept, weights, biases):
    frames_out = (first_maps.shape[0] - 1) // 2
    bins = first_maps.shape[1]
    channels = first_maps.shape[2]
    padded = jnp.pad(first_maps, ((0, 0), (1, 1), (0, 0)))
    kept_half = kept.astype(jnp.bfloat16)
    summed = jnp.zeros((frames_out * (bins // 2), weights.shape[3]), jnp.float32)
    for step_time in range(3):
        for step_bin in range(3):
            tapped = padded[step_time:step_time + 2 * frames_out - 1:2, step_bin:step_bin + bins - 1:2]
            if step_time == 0:
                tapped = tapped * kept_half[:, None, None]
            summed = summed + jnp.dot(tapped.reshape(frames_out * (bins // 2), channels), weights[step_time, step_bin], preferred_element_type=jnp.float32)
    activated = jax.nn.relu(summed + biases).astype(jnp.bfloat16)
    return activated.reshape(frames_out, bins // 2, weights.shape[3])

def group_forward(raw_rows, lengths_row, conv1_weight, conv1_bias, conv2_weight, conv2_bias, proj_weight, proj_bias, norm_gain, qkv_weight, out_weight):
    group_len = raw_rows.shape[0] // 4
    positions = jnp.arange(group_len, dtype=jnp.int32)
    starts, segment = segment_info(lengths_row, positions, group_len)
    kept = 1.0 - starts.astype(jnp.float32)
    widened = jnp.concatenate([jnp.zeros((3, raw_rows.shape[1]), jnp.float32), raw_rows.astype(jnp.float32)], axis=0)
    first_maps = first_conv(widened, kept, conv1_weight, conv1_bias)
    second_maps = second_conv(first_maps, kept, conv2_weight, conv2_bias)
    flattened = second_maps.transpose(0, 2, 1).reshape(group_len, -1)
    frames = (jnp.dot(flattened, proj_weight, preferred_element_type=jnp.float32) + proj_bias).astype(jnp.bfloat16)
    values32 = frames.astype(jnp.float32)
    average = lax.optimization_barrier(jnp.mean(values32, axis=1, keepdims=True))
    centered = values32 - average
    variance = lax.optimization_barrier(jnp.mean(centered * centered, axis=1, keepdims=True))
    normed = (centered * lax.rsqrt(variance + 1e-05) * norm_gain).astype(jnp.bfloat16)
    width = qkv_weight.shape[0]
    projected = jnp.dot(normed, qkv_weight.reshape(width, 3 * width), preferred_element_type=jnp.float32).astype(jnp.bfloat16)
    head_count = width // HEAD

    def split_heads(block):
        return block.reshape(group_len, head_count, HEAD).transpose(1, 0, 2)
    query = split_heads(projected[:, :width])
    keys = split_heads(projected[:, width:2 * width])
    values = split_heads(projected[:, 2 * width:])
    same = segment[:, None] == segment[None, :]
    scale = 1.0 / math.sqrt(HEAD)

    def one_head(operands):
        query_head, key_head, value_head = operands
        scores = jnp.dot(query_head, key_head.T, preferred_element_type=jnp.float32) * scale
        scores = jnp.where(same, scores, -1e+30)
        highest = lax.optimization_barrier(jnp.max(scores, axis=1, keepdims=True))
        weight = jnp.where(same, jnp.exp(scores - highest), 0.0)
        denominator = lax.optimization_barrier(jnp.sum(weight, axis=1))
        numerator = jnp.dot(weight.astype(jnp.bfloat16), value_head, preferred_element_type=jnp.float32)
        return numerator / denominator[:, None]
    context = lax.map(one_head, (query, keys, values))
    context = context.transpose(1, 0, 2).reshape(group_len, width).astype(jnp.bfloat16)
    branch = jnp.dot(context, out_weight, preferred_element_type=jnp.float32)
    return (values32 + branch).astype(jnp.bfloat16)

def reference(features, lengths, conv1_weight, conv1_bias, conv2_weight, conv2_bias, proj_weight, proj_bias, norm_gain, qkv_weight, out_weight):

    def one_group(operands):
        raw_rows, lengths_row = operands
        return group_forward(raw_rows, lengths_row, conv1_weight, conv1_bias, conv2_weight, conv2_bias, proj_weight, proj_bias, norm_gain, qkv_weight, out_weight)
    return lax.map(one_group, (features, lengths))
```

```python
import math

import jax
import jax.numpy as jnp
import numpy as np
from jax import lax
from jax.experimental import pallas as pl
from jax.experimental.pallas import tpu as pltpu
from jax.sharding import PartitionSpec as P

MESH = pl.DeviceIdType.MESH
BF16 = jnp.bfloat16
F32 = jnp.float32

SIDE = 4
BLOCKS = SIDE * SIDE
FRAMES = 128
HALF = 64
BINS = 32
UTTS = 12
WIDTH = 1536
LOCAL = 768
HEAD = 64
EVEN = 144
ROWS = EVEN + FRAMES
PADDED = 584
TILES = 8
CUT = 256
CUTS = WIDTH // CUT
REACH = 2
SPAN = (2 * REACH + 1) * FRAMES
NEAR = (-2, -1, 1, 2)


def dot(a, b):
    return jnp.dot(a, b, preferred_element_type=F32)


def body(
    lengths_ref,
    feat_ref,
    w1_ref,
    b1_ref,
    w2_ref,
    b2_ref,
    wp_ref,
    pb_ref,
    gain_ref,
    qkv_ref,
    wo_ref,
    out_ref,
    halo,
    padded,
    picker,
    base,
    taps,
    patches,
    w2_even,
    w2_odd,
    fe,
    fo,
    w_all,
    maps_out,
    maps_in,
    part,
    sib_out,
    sib_in,
    tot,
    rs_out,
    rs_in,
    frames_mine,
    frames_cols,
    normed,
    qkv_w,
    out_w,
    query,
    keys,
    values,
    bias_mask,
    context,
    br_out,
    br_in,
    w2_sem,
    qkv_sem,
    out_sem,
    halo_send,
    halo_recv,
    w_send,
    w_recv,
    m_send,
    m_recv,
    sib_send,
    sib_recv,
    rs_send,
    rs_recv,
    fr_send,
    fr_recv,
    n_send,
    n_recv,
    own_send,
    own_recv,
    fw_send,
    fw_recv,
    br_send,
    br_recv,
):
    phase = lax.axis_index("phase")
    block = lax.axis_index("seq")
    x = block % SIDE
    y = block // SIDE
    other = 1 - phase

    def row_peer(dx):
        return y * SIDE + (x + dx) % SIDE

    def column_peer(dy):
        return ((y + dy) % SIDE) * SIDE + x

    def near_peer(d):
        return (block + d + BLOCKS) % BLOCKS

    def remote(src, dst, send, recv, target):
        return pltpu.make_async_remote_copy(
            src_ref=src,
            dst_ref=dst,
            send_sem=send,
            recv_sem=recv,
            device_id=target,
            device_id_type=MESH,
        )

    local_w2 = []
    for b in range(3):
        rows = pl.ds(b * 256, 256)
        local_w2.append(
            pltpu.make_async_copy(w2_ref.at[0, b], w2_even.at[rows, pl.ds(0, 128)], w2_sem.at[b])
        )
        local_w2.append(
            pltpu.make_async_copy(
                w2_ref.at[2, b], w2_even.at[rows, pl.ds(128, 128)], w2_sem.at[3 + b]
            )
        )
        local_w2.append(pltpu.make_async_copy(w2_ref.at[1, b], w2_odd.at[rows], w2_sem.at[6 + b]))
    for copy in local_w2:
        copy.start()
    qkv_copy = pltpu.make_async_copy(qkv_ref, qkv_w, qkv_sem)
    out_copy = pltpu.make_async_copy(wo_ref, out_w, out_sem)
    qkv_copy.start()
    out_copy.start()

    barrier = pltpu.get_barrier_semaphore()
    peers = [{"phase": other}]
    peers += [{"seq": row_peer(dx)} for dx in range(1, SIDE)]
    peers += [{"seq": column_peer(dy)} for dy in range(1, SIDE)]
    peers += [{"seq": near_peer(d)} for d in NEAR]
    for peer in peers:
        pl.semaphore_signal(barrier, inc=1, device_id=peer, device_id_type=MESH)

    out_row = lax.broadcasted_iota(jnp.int32, (256, 256), 0)
    in_row = lax.broadcasted_iota(jnp.int32, (256, 256), 1)
    reorder = jnp.where(in_row == (out_row & 7) * BINS + (out_row >> 3), 1.0, 0.0).astype(BF16)
    own_rows = pl.ds(pl.multiple_of(y * 32, 32), 32)
    for n in range(CUTS):
        cols = slice(n * CUT, (n + 1) * CUT)
        moved = dot(reorder, wp_ref[:, cols]).astype(BF16)
        for g in range(TILES):
            w_all[g, own_rows, cols] = moved[g * 32 : (g + 1) * 32]

    pl.semaphore_wait(barrier, len(peers))

    halo_copy = remote(
        feat_ref.at[pl.ds(496, 16)], halo, halo_send, halo_recv, {"seq": near_peer(1)}
    )
    halo_copy.start()
    w_copies = []
    for dy in range(1, SIDE):
        w_copies.append(
            remote(
                w_all.at[:, own_rows, :],
                w_all.at[:, own_rows, :],
                w_send.at[dy - 1],
                w_recv.at[dy - 1],
                {"seq": column_peer(dy)},
            )
        )
    for k in (0, 2, 1):
        w_copies[k].start()

    offsets = []
    running = jnp.int32(0)
    for i in range(UTTS):
        offsets.append(running)
        running = running + lengths_ref[0, i]
    place = lax.broadcasted_iota(jnp.int32, (FRAMES, 128), 0) + block * FRAMES
    starts = place == offsets[0]
    seg_query = jnp.where(place >= offsets[0], 1, 0)
    for off in offsets[1:]:
        starts = starts | (place == off)
        seg_query = seg_query + jnp.where(place >= off, 1, 0)
    kept = jnp.where(starts, 0.0, 1.0)
    key_place = lax.broadcasted_iota(jnp.int32, (8, SPAN), 1) + (block - REACH) * FRAMES
    seg_key = jnp.where(key_place >= offsets[0], 1, 0)
    for off in offsets[1:]:
        seg_key = seg_key + jnp.where(key_place >= off, 1, 0)
    seg_key = jnp.where((key_place >= 0) & (key_place < BLOCKS * FRAMES), seg_key, 0)
    for j in range(SPAN // 128):
        cols = slice(j * 128, (j + 1) * 128)
        bias_mask[:, cols] = jnp.where(seg_query == seg_key[0:1, cols], 0.0, -1e30)

    base[...] = jnp.zeros_like(base)
    for a in range(3):
        for b in range(3):
            for shift in range(3):
                row = 8 * a + 2 * shift + b
                base[row : row + 1, shift * 256 : (shift + 1) * 256] = w1_ref[a, b : b + 1, :]
    bias1 = b1_ref[...]
    high = bias1.astype(BF16).astype(F32)
    middle = (bias1 - high).astype(BF16).astype(F32)
    for k, piece in enumerate((high, middle, bias1 - high - middle)):
        base[24 + k : 25 + k, 0:256] = piece
        base[8 * k + 7 : 8 * k + 8, 256:512] = piece
        base[8 * k + 7 : 8 * k + 8, 512:768] = piece
    taps[...] = jnp.zeros_like(taps)
    for r in range(4):
        taps[r, 32 * r : 32 * r + 32, :] = base[...].astype(BF16)

    bins_in = lax.broadcasted_iota(jnp.int32, (128, BINS * 32), 0)
    lane = lax.broadcasted_iota(jnp.int32, (128, BINS * 32), 1)
    tap_bin = lane & 7
    tap_time = (lane >> 3) & 3
    hit = (bins_in == ((lane >> 5) * 4 + tap_bin - 3)) & (tap_bin < 7)
    for a in range(3):
        picker[a * 128 : (a + 1) * 128, :] = jnp.where(hit & (tap_time == a), 1.0, 0.0).astype(BF16)
    lane1 = lax.broadcasted_iota(jnp.int32, (1, BINS * 32), 1)
    low = lane1 & 31
    constant = ((low & 7) == 7) & (low < 24)
    constant = constant | ((low >= 24) & (low < 27) & (lane1 >= 32))
    constant = jnp.where(constant, 1.0, 0.0)

    padded[8:520, :] = feat_ref[...].astype(F32)
    padded[520:PADDED, :] = jnp.zeros((PADDED - 520, 128), F32)
    halo_copy.wait_recv()
    first = jnp.where(block > 0, 1.0, 0.0)
    padded[0:8, :] = halo[...].astype(F32)[8:16] * first
    even = [padded[pl.ds(5 + a, EVEN, stride=4), :] for a in range(3)]
    odd = [padded[pl.ds(7 + a, FRAMES, stride=4), :] for a in range(3)]
    odd[0] = odd[0] * kept
    gathered = jnp.concatenate(
        [jnp.concatenate(even, axis=1), jnp.concatenate(odd, axis=1)], axis=0
    ).astype(BF16)
    for k in range(4):
        cols = slice(k * 256, (k + 1) * 256)
        made = (dot(gathered, picker[:, cols]) + constant[:, cols]).astype(BF16)
        patches[2 * k] = made[:, 0:128]
        patches[2 * k + 1] = made[:, 128:256]

    for copy in local_w2:
        copy.wait()

    lane_slot = (lax.broadcasted_iota(jnp.int32, (FRAMES, 128), 1) >> 3) & 3
    bias2 = b2_ref[...]

    def maps_copy(dx, g):
        return remote(
            maps_out.at[(x + dx) % SIDE, g],
            maps_in.at[x, g],
            m_send.at[dx - 1, g],
            m_recv.at[dx - 1, g],
            {"seq": row_peer(dx)},
        )

    def convolve(g, carry):
        patch = patches[g]
        for r in range(4):
            for shift in range(3):
                cols = slice(shift * 256, (shift + 1) * 256)
                first_map = jnp.maximum(dot(patch, taps[r, :, cols]), 0.0).astype(BF16)
                fe[r * EVEN : (r + 1) * EVEN, cols] = first_map[:EVEN]
                fo[r * FRAMES : (r + 1) * FRAMES, cols] = first_map[EVEN:]
        second = []
        for r in range(4):
            sums = dot(fe[r * EVEN : (r + 1) * EVEN, :], w2_even[...])
            sums_odd = dot(fo[r * FRAMES : (r + 1) * FRAMES, :], w2_odd[...])
            later = pltpu.roll(sums[:, 128:256], EVEN - 1, 0)[:FRAMES]
            total = sums[:FRAMES, 0:128] * kept + later + sums_odd + bias2
            second.append(jnp.maximum(total, 0.0))
        for to in range(SIDE):
            mixed = second[to]
            for r in range(4):
                if r != to:
                    turned = pltpu.roll(second[r], (8 * (r - to)) % 128, 1)
                    mixed = jnp.where(lane_slot == r, turned, mixed)
            maps_out[to, g] = mixed.astype(BF16)
        for dx in (2, 1, 3):
            maps_copy(dx, g).start()
        return carry

    lax.fori_loop(0, TILES, convolve, 0)

    for g in range(TILES):
        maps_in[x, g] = maps_out[x, g]

    def maps_wait(g, carry):
        for dx in range(1, SIDE):
            maps_copy(dx, g).wait_recv()
        return carry

    lax.fori_loop(0, TILES, maps_wait, 0)
    for copy in w_copies:
        copy.wait_recv()

    mine = pl.ds(pl.multiple_of(phase * HALF, HALF), HALF)
    theirs = pl.ds(pl.multiple_of(other * HALF, HALF), HALF)

    def sib_copy(n):
        return remote(
            sib_out.at[n], sib_in.at[n], sib_send.at[n], sib_recv.at[n], {"phase": other}
        )

    def rs_copy(dx, n):
        return remote(
            rs_out.at[n, (x + dx) % SIDE],
            rs_in.at[dx - 1, n],
            rs_send.at[dx - 1, n],
            rs_recv.at[dx - 1, n],
            {"seq": row_peer(dx)},
        )

    def project(n):
        cols = pl.ds(pl.multiple_of(n * CUT, CUT), CUT)
        maps = jnp.concatenate(
            [
                jnp.concatenate([maps_in[s, g] for g in range(TILES)], axis=1)
                for s in range(SIDE)
            ],
            axis=0,
        )
        weights = w_all[:, :, cols].reshape(TILES * 128, CUT)
        part[n] = dot(maps, weights).reshape(SIDE, FRAMES, CUT)
        sib_out[n] = part[n, :, theirs, :].astype(BF16)
        sib_copy(n).start()

    def pass_on(n):
        sib_copy(n).wait_recv()
        both = part[n, :, mine, :] + sib_in[n].astype(F32)
        tot[n] = both
        rs_out[n] = both.astype(BF16)
        for dx in (2, 1, 3):
            rs_copy(dx, n).start()

    def project_step(n, carry):
        @pl.when(n < CUTS)
        def _():
            project(n)

        @pl.when(n >= 2)
        def _():
            pass_on(n - 2)

        return carry

    lax.fori_loop(0, CUTS + 2, project_step, 0)

    for n in range(CUTS):
        cols = slice(n * CUT, (n + 1) * CUT)
        for dx in range(1, SIDE):
            rs_copy(dx, n).wait_recv()
        total = tot[n, x]
        for dx in range(1, SIDE):
            total = total + rs_in[dx - 1, n].astype(F32)
        frames_mine[:, cols] = (total + pb_ref[:, cols]).astype(BF16)
    frames_copy = remote(
        frames_mine.at[:, pl.ds(pl.multiple_of(other * LOCAL, LOCAL), LOCAL)],
        frames_cols.at[mine, :],
        fr_send,
        fr_recv,
        {"phase": other},
    )
    frames_copy.start()
    numbers = frames_mine[...].astype(F32)
    average = jnp.mean(numbers, axis=1, keepdims=True)
    centered = numbers - average
    variance = jnp.mean(centered * centered, axis=1, keepdims=True)
    own_slot = pl.ds(pl.multiple_of(REACH * FRAMES + phase * HALF, HALF), HALF)
    normed[own_slot, :] = (centered * lax.rsqrt(variance + 1e-05) * gain_ref[...]).astype(BF16)

    def slot(d):
        return pl.ds(pl.multiple_of((REACH + d) * FRAMES + phase * HALF, HALF), HALF)

    near = []
    forward = []
    for k, d in enumerate(NEAR):
        near.append(
            remote(
                normed.at[own_slot, :],
                normed.at[slot(d), :],
                n_send.at[k],
                n_recv.at[k],
                {"seq": near_peer(-d)},
            )
        )
        forward.append(
            remote(
                normed.at[slot(d), :],
                normed.at[slot(d), :],
                fw_send.at[k],
                fw_recv.at[k],
                {"phase": other},
            )
        )
    own_copy = remote(
        normed.at[own_slot, :], normed.at[own_slot, :], own_send, own_recv, {"phase": other}
    )
    for k in (0, 3, 1, 2):
        near[k].start()
    own_copy.start()
    frames_cols[mine, :] = frames_mine[:, pl.ds(pl.multiple_of(phase * LOCAL, LOCAL), LOCAL)]
    qkv_copy.wait()
    out_copy.wait()
    own_copy.wait_recv()

    def keys_values(low, rows):
        block_rows = normed[low : low + rows, :]
        for n in range(3):
            cols = slice(n * CUT, (n + 1) * CUT)
            keys[low : low + rows, cols] = dot(block_rows, qkv_w[1, :, cols]).astype(BF16)
            values[low : low + rows, cols] = dot(block_rows, qkv_w[2, :, cols]).astype(BF16)

    own_low = REACH * FRAMES
    own_block = normed[own_low : own_low + FRAMES, :]
    for n in range(3):
        cols = slice(n * CUT, (n + 1) * CUT)
        made = dot(own_block, qkv_w[0, :, cols]).astype(BF16)
        query[:, cols] = made * jnp.asarray(1.0 / math.sqrt(HEAD), BF16)
    keys_values(own_low, FRAMES)
    for k in (1, 2):
        near[k].wait_recv()
        forward[k].start()
    for k in (1, 2):
        forward[k].wait_recv()
    keys_values(FRAMES, FRAMES)
    keys_values(3 * FRAMES, FRAMES)
    for k in (0, 3):
        near[k].wait_recv()
        forward[k].start()
    for k in (0, 3):
        forward[k].wait_recv()
    keys_values(0, FRAMES)
    keys_values(4 * FRAMES, FRAMES)

    lane_low = lax.broadcasted_iota(jnp.int32, (FRAMES, 128), 1) < HEAD

    def attend(pair, carry):
        cols = pl.ds(pl.multiple_of(pair * 128, 128), 128)
        both = query[:, cols]
        zero = jnp.zeros_like(both)
        stacked = jnp.concatenate(
            [jnp.where(lane_low, both, zero), jnp.where(lane_low, zero, both)], axis=0
        )
        scores = lax.dot_general(
            stacked, keys[:, cols], (((1,), (1,)), ((), ())), preferred_element_type=F32
        )
        mask = bias_mask[...]
        scores = scores + jnp.concatenate([mask, mask], axis=0)
        highest = jnp.max(scores, axis=1, keepdims=True)
        weight = jnp.exp(scores - highest)
        denominator = jnp.sum(weight, axis=1, keepdims=True)
        mixed = dot(weight.astype(BF16), values[:, cols]) / denominator
        context[:, cols] = jnp.where(lane_low, mixed[:FRAMES], mixed[FRAMES:]).astype(BF16)
        return carry

    lax.fori_loop(0, LOCAL // 128, attend, 0)

    def br_copy(n):
        return remote(br_out.at[n], br_in.at[n], br_send.at[n], br_recv.at[n], {"phase": other})

    for n in range(3):
        cols = pl.ds(pl.multiple_of(other * LOCAL + n * CUT, CUT), CUT)
        br_out[n] = dot(context[...], out_w[:, cols]).astype(BF16)
        br_copy(n).start()
    frames_copy.wait_recv()
    for n in range(3):
        cols = pl.ds(pl.multiple_of(phase * LOCAL + n * CUT, CUT), CUT)
        here = slice(n * CUT, (n + 1) * CUT)
        total = frames_cols[:, here].astype(F32) + dot(context[...], out_w[:, cols])
        br_copy(n).wait_recv()
        out_ref[:, here] = (total + br_in[n].astype(F32)).astype(BF16)

    halo_copy.wait_send()
    for copy in w_copies:
        copy.wait_send()

    def maps_sent(g, carry):
        for dx in range(1, SIDE):
            maps_copy(dx, g).wait_send()
        return carry

    lax.fori_loop(0, TILES, maps_sent, 0)

    def sums_sent(n, carry):
        sib_copy(n).wait_send()
        for dx in range(1, SIDE):
            rs_copy(dx, n).wait_send()
        return carry

    lax.fori_loop(0, CUTS, sums_sent, 0)
    frames_copy.wait_send()
    own_copy.wait_send()
    for k in range(len(NEAR)):
        near[k].wait_send()
        forward[k].wait_send()
    for n in range(3):
        br_copy(n).wait_send()


def local(
    features,
    lengths,
    conv1_weight,
    conv1_bias,
    conv2_weight,
    conv2_bias,
    proj_weight,
    proj_bias,
    norm_gain,
    qkv_weight,
    out_weight,
):
    vmem = pl.BlockSpec(memory_space=pltpu.VMEM)
    smem = pl.BlockSpec(memory_space=pltpu.SMEM)
    hbm = pl.BlockSpec(memory_space=pl.ANY)
    dma = pltpu.SemaphoreType.DMA
    scratch = [
        pltpu.VMEM((16, 128), BF16),
        pltpu.VMEM((PADDED, 128), F32),
        pltpu.VMEM((384, BINS * 32), BF16),
        pltpu.VMEM((32, 768), F32),
        pltpu.VMEM((4, 128, 768), BF16),
        pltpu.VMEM((TILES, ROWS, 128), BF16),
        pltpu.VMEM((768, 256), BF16),
        pltpu.VMEM((768, 128), BF16),
        pltpu.VMEM((4 * EVEN, 768), BF16),
        pltpu.VMEM((4 * FRAMES, 768), BF16),
        pltpu.VMEM((TILES, 128, WIDTH), BF16),
        pltpu.VMEM((SIDE, TILES, FRAMES, 128), BF16),
        pltpu.VMEM((SIDE, TILES, FRAMES, 128), BF16),
        pltpu.VMEM((CUTS, SIDE, FRAMES, CUT), F32),
        pltpu.VMEM((CUTS, SIDE, HALF, CUT), BF16),
        pltpu.VMEM((CUTS, SIDE, HALF, CUT), BF16),
        pltpu.VMEM((CUTS, SIDE, HALF, CUT), F32),
        pltpu.VMEM((CUTS, SIDE, HALF, CUT), BF16),
        pltpu.VMEM((SIDE - 1, CUTS, HALF, CUT), BF16),
        pltpu.VMEM((HALF, WIDTH), BF16),
        pltpu.VMEM((FRAMES, LOCAL), BF16),
        pltpu.VMEM((SPAN, WIDTH), BF16),
        pltpu.VMEM((3, WIDTH, LOCAL), BF16),
        pltpu.VMEM((LOCAL, WIDTH), BF16),
        pltpu.VMEM((FRAMES, LOCAL), BF16),
        pltpu.VMEM((SPAN, LOCAL), BF16),
        pltpu.VMEM((SPAN, LOCAL), BF16),
        pltpu.VMEM((FRAMES, SPAN), F32),
        pltpu.VMEM((FRAMES, LOCAL), BF16),
        pltpu.VMEM((3, FRAMES, CUT), BF16),
        pltpu.VMEM((3, FRAMES, CUT), BF16),
        dma((9,)),
        dma,
        dma,
        dma,
        dma,
        dma((3,)),
        dma((3,)),
        dma((3, TILES)),
        dma((3, TILES)),
        dma((CUTS,)),
        dma((CUTS,)),
        dma((3, CUTS)),
        dma((3, CUTS)),
        dma,
        dma,
        dma((4,)),
        dma((4,)),
        dma,
        dma,
        dma((4,)),
        dma((4,)),
        dma((3,)),
        dma((3,)),
    ]
    encoded = pl.pallas_call(
        body,
        out_shape=jax.ShapeDtypeStruct((FRAMES, LOCAL), BF16),
        in_specs=[smem, vmem, vmem, vmem, hbm, vmem, vmem, vmem, vmem, hbm, hbm],
        out_specs=vmem,
        scratch_shapes=scratch,
        compiler_params=pltpu.CompilerParams(
            collective_id=0, has_side_effects=True, vmem_limit_bytes=48 * 1024 * 1024
        ),
    )(
        lengths,
        features[0],
        conv1_weight,
        conv1_bias[None],
        conv2_weight,
        conv2_bias[None],
        proj_weight,
        proj_bias[None],
        norm_gain[None],
        qkv_weight.transpose(1, 0, 2),
        out_weight,
    )
    return encoded[None]


def solution(mesh):
    in_specs = (
        P("batch", "seq", None),
        P("batch", None),
        P(),
        P(),
        P(None, None, None, "phase"),
        P("phase"),
        P(("phase", "seq"), None),
        P(),
        P(),
        P(None, None, "phase"),
        P("phase", None),
    )
    out_specs = P("batch", "seq", "phase")
    return jax.shard_map(local, mesh=mesh, in_specs=in_specs, out_specs=out_specs, check_vma=False)
```

```python
import math

import jax
import jax.numpy as jnp
from jax import lax
from jax.experimental import pallas as pl
from jax.experimental.pallas import tpu as pltpu
from jax.sharding import PartitionSpec as P

MESH = pl.DeviceIdType.MESH
BF16 = jnp.bfloat16
F32 = jnp.float32

SIDE = 4
BLOCKS = SIDE * SIDE
FRAMES = 128
HALF = 64
QUARTER = 32
BINS = 32
UTTS = 12
WIDTH = 1536
LOCAL = 768
HEAD = 64
EVEN = 144
ROWS = EVEN + FRAMES
PADDED = 584
TILES = 8
CUT = 256
CUTS = WIDTH // CUT
REACH = 2
SPAN = (2 * REACH + 1) * FRAMES
NEAR = (-2, -1, 1, 2)


def dot(a, b):
    return jnp.dot(a, b, preferred_element_type=F32)


def body(
    lengths_ref,
    feat_hbm,
    w1_hbm,
    b1_hbm,
    w2_ref,
    b2_hbm,
    wp_hbm,
    pb_hbm,
    gain_hbm,
    qkv_ref,
    wo_ref,
    out_ref,
    feat_ref,
    w1_ref,
    b1_ref,
    b2_ref,
    wp_ref,
    pb_ref,
    gain_ref,
    halo,
    padded,
    picker,
    base,
    taps,
    patches,
    w2_even,
    w2_odd,
    first_even,
    first_odd,
    w_all,
    maps_out,
    maps_in,
    part,
    sib_out,
    sib_in,
    tot,
    rs_out,
    rs_in,
    frames_mine,
    frames_cols,
    normed,
    qkv_w,
    out_w,
    query,
    keys,
    values,
    bias_mask,
    context,
    br_out,
    br_in,
    in_sem,
    w2_sem,
    qkv_sem,
    out_sem,
    halo_send,
    halo_recv,
    wy_send,
    wy_recv,
    wz_send,
    wz_recv,
    m_send,
    m_recv,
    sib_send,
    sib_recv,
    rs_send,
    rs_recv,
    fr_send,
    fr_recv,
    n_send,
    n_recv,
    s_send,
    s_recv,
    br_send,
    br_recv,
):
    phase = lax.axis_index("phase")
    block = lax.axis_index("seq")
    x = block % SIDE
    y = block // SIDE
    plane = lax.axis_index("batch")
    planes = lax.axis_size("batch")
    other = 1 - phase

    def row_of(ref):
        return jnp.concatenate([ref[k : k + 1, :] for k in range(WIDTH // 128)], axis=1)

    def row_peer(dx):
        return y * SIDE + (x + dx) % SIDE

    def column_peer(dy):
        return ((y + dy + SIDE) % SIDE) * SIDE + x

    def plane_peer(dz):
        return (plane + dz + planes) % planes

    def near_peer(d):
        return (block + d + BLOCKS) % BLOCKS

    def remote(src, dst, send, recv, target):
        return pltpu.make_async_remote_copy(
            src_ref=src,
            dst_ref=dst,
            send_sem=send,
            recv_sem=recv,
            device_id=target,
            device_id_type=MESH,
        )

    inputs = [
        pltpu.make_async_copy(source, target, in_sem.at[k])
        for k, (source, target) in enumerate(
            (
                (wp_hbm, wp_ref),
                (feat_hbm, feat_ref),
                (w1_hbm, w1_ref),
                (b1_hbm, b1_ref),
                (b2_hbm, b2_ref),
                (pb_hbm, pb_ref),
                (gain_hbm, gain_ref),
            )
        )
    ]
    for copy in inputs:
        copy.start()
    local_w2 = []
    for b in range(3):
        rows = pl.ds(b * 256, 256)
        local_w2.append(
            pltpu.make_async_copy(w2_ref.at[0, b], w2_even.at[rows, pl.ds(0, 128)], w2_sem.at[b])
        )
        local_w2.append(
            pltpu.make_async_copy(
                w2_ref.at[2, b], w2_even.at[rows, pl.ds(128, 128)], w2_sem.at[3 + b]
            )
        )
        local_w2.append(pltpu.make_async_copy(w2_ref.at[1, b], w2_odd.at[rows], w2_sem.at[6 + b]))
    for copy in local_w2:
        copy.start()
    qkv_copy = pltpu.make_async_copy(qkv_ref, qkv_w, qkv_sem)
    out_copy = pltpu.make_async_copy(wo_ref, out_w, out_sem)
    qkv_copy.start()
    out_copy.start()

    barrier = pltpu.get_barrier_semaphore()
    peers = [{"phase": other}]
    peers += [{"seq": row_peer(dx)} for dx in range(1, SIDE)]
    peers += [{"seq": column_peer(dy)} for dy in (1, 3)]
    peers += [{"batch": plane_peer(dz)} for dz in (1, -1)]
    peers += [{"seq": near_peer(d)} for d in (1, -1)]
    for peer in peers:
        pl.semaphore_signal(barrier, inc=1, device_id=peer, device_id_type=MESH)

    out_row = lax.broadcasted_iota(jnp.int32, (256, 256), 0)
    in_row = lax.broadcasted_iota(jnp.int32, (256, 256), 1)
    reorder = jnp.where(in_row == (out_row & 7) * BINS + (out_row >> 3), 1.0, 0.0).astype(BF16)
    own_rows = pl.ds(pl.multiple_of(y * 32, 32), 32)
    inputs[0].wait()
    for n in range(CUTS):
        cols = slice(n * CUT, (n + 1) * CUT)
        moved = dot(reorder, wp_ref[:, cols]).astype(BF16)
        for g in range(TILES):
            w_all[g, own_rows, cols] = moved[g * 32 : (g + 1) * 32]

    inputs[1].wait()
    pl.semaphore_wait(barrier, len(peers))

    halo_copy = remote(
        feat_ref.at[pl.ds(496, 16)], halo, halo_send, halo_recv, {"seq": near_peer(1)}
    )
    halo_copy.start()
    drain = [halo_copy.wait_send]
    half_low = (plane % 2) * 4
    pieces = [
        (-1, 0, 1),
        (1, 1, -1),
        (-1, 1, -1),
        (1, 0, 1),
        (2, 0, 1),
        (2, 1, -1),
    ]

    def w_piece(dy, part_of, low):
        rows = pl.ds(pl.multiple_of(((y + dy + SIDE) % SIDE) * 32, 32), 32)
        return w_all.at[pl.ds(low + 2 * part_of, 2), rows, :]

    def w_along_y(k):
        dy, part_of, _ = pieces[k]
        step = -1 if dy == -1 or (dy == 2 and part_of == 0) else 1
        mine = w_piece(dy - step, part_of, half_low)
        return remote(
            mine, mine, wy_send.at[k], wy_recv.at[k], {"seq": column_peer(-step)}
        )

    def w_along_z(k):
        dy, part_of, dz = pieces[k]
        mine = w_piece(dy, part_of, half_low)
        return remote(mine, mine, wz_send.at[k], wz_recv.at[k], {"batch": plane_peer(dz)})

    def w_sent():
        for k in range(6):
            w_along_y(k).wait_send()
            w_along_z(k).wait_send()

    drain.append(w_sent)
    for k in range(4):
        w_along_y(k).start()

    def w_step(step):
        for k in (2 * step, 2 * step + 1):
            w_along_y(k).wait_recv()
            if step == 0:
                w_along_y(4 + k).start()
            w_along_z(k).start()

    offsets = []
    running = jnp.int32(0)
    for i in range(UTTS):
        offsets.append(running)
        running = running + lengths_ref[0, i]
    place = lax.broadcasted_iota(jnp.int32, (FRAMES, 128), 0) + block * FRAMES
    starts = place == offsets[0]
    seg_query = jnp.where(place >= offsets[0], 1, 0)
    for off in offsets[1:]:
        starts = starts | (place == off)
        seg_query = seg_query + jnp.where(place >= off, 1, 0)
    kept = jnp.where(starts, 0.0, 1.0)
    key_place = lax.broadcasted_iota(jnp.int32, (8, SPAN), 1) + (block - REACH) * FRAMES
    seg_key = jnp.where(key_place >= offsets[0], 1, 0)
    for off in offsets[1:]:
        seg_key = seg_key + jnp.where(key_place >= off, 1, 0)
    seg_key = jnp.where((key_place >= 0) & (key_place < BLOCKS * FRAMES), seg_key, 0)
    for j in range(SPAN // 128):
        cols = slice(j * 128, (j + 1) * 128)
        bias_mask[:, cols] = jnp.where(seg_query == seg_key[0:1, cols], 0.0, -1e30)

    for copy in inputs[2:]:
        copy.wait()
    base[...] = jnp.zeros_like(base)

    def two_pieces(value):
        high = value.astype(BF16).astype(F32)
        return high, value - high

    for a in range(3):
        pair = two_pieces(w1_ref[a])
        for b in range(3):
            for shift in range(2):
                for k in range(2):
                    row = 15 * k + 5 * a + 2 * shift + b
                    base[row : row + 1, shift * 256 : (shift + 1) * 256] = pair[k][b : b + 1, :]
    pair = two_pieces(jnp.concatenate([b1_ref[0:1, :], b1_ref[1:2, :]], axis=1))
    for k in range(2):
        for shift in range(2):
            base[30 + k : 31 + k, shift * 256 : (shift + 1) * 256] = pair[k]
    taps[...] = jnp.zeros_like(taps)
    for r in range(4):
        taps[r, 32 * r : 32 * r + 32, :] = base[...].astype(BF16)

    lane = lax.broadcasted_iota(jnp.int32, (1, BINS * 32), 1)
    low = lane & 31
    tap = jnp.where(low >= 15, low - 15, low)
    tap_time = jnp.where(tap >= 5, 1, 0) + jnp.where(tap >= 10, 1, 0)
    tap_bin = (lane >> 5) * 4 + (tap - 5 * tap_time) - 1
    wanted = jnp.where((low < 30) & (tap_bin >= 0), tap_time * 128 + tap_bin, -1)
    constant = jnp.where(low >= 30, 1.0, 0.0)
    for a in range(3):
        bins_in = lax.broadcasted_iota(jnp.int32, (128, BINS * 32), 0) + a * 128
        picker[a * 128 : (a + 1) * 128, :] = jnp.where(bins_in == wanted, 1.0, 0.0).astype(BF16)

    padded[8:520, :] = feat_ref[...].astype(F32)
    padded[520:PADDED, :] = jnp.zeros((PADDED - 520, 128), F32)
    halo_copy.wait_recv()
    first = jnp.where(block > 0, 1.0, 0.0)
    padded[0:8, :] = halo[...].astype(F32)[8:16] * first
    even = [padded[pl.ds(5 + a, EVEN, stride=4), :] for a in range(3)]
    odd = [padded[pl.ds(7 + a, FRAMES, stride=4), :] for a in range(3)]
    odd[0] = odd[0] * kept
    gathered = jnp.concatenate(
        [jnp.concatenate(even, axis=1), jnp.concatenate(odd, axis=1)], axis=0
    ).astype(BF16)
    for k in range(4):
        cols = slice(k * 256, (k + 1) * 256)
        made = (dot(gathered, picker[:, cols]) + constant[:, cols]).astype(BF16)
        patches[2 * k] = made[:, 0:128]
        patches[2 * k + 1] = made[:, 128:256]

    for copy in local_w2:
        copy.wait()

    lane_slot = (lax.broadcasted_iota(jnp.int32, (FRAMES, 128), 1) >> 3) & 3
    bias2 = b2_ref[...]

    def maps_copy(dx, g):
        return remote(
            maps_out.at[(x + dx) % SIDE, g],
            maps_in.at[x, g],
            m_send.at[dx - 1, g],
            m_recv.at[dx - 1, g],
            {"seq": row_peer(dx)},
        )

    def convolve(g, carry):
        patch = patches[g]
        first_odd[0] = first_odd[4]
        for r in range(4):
            first_even[r] = jnp.maximum(dot(patch, taps[r, :, 0:256]), 0.0).astype(BF16)
            first_odd[r + 1] = jnp.maximum(dot(patch, taps[r, :, 256:512]), 0.0).astype(BF16)

        def three_bins(rows):
            return jnp.concatenate(
                [
                    jnp.concatenate(
                        [first_odd[r, rows], first_even[r, rows], first_odd[r + 1, rows]], axis=1
                    )
                    for r in range(4)
                ],
                axis=0,
            )

        sums = dot(three_bins(slice(0, EVEN)), w2_even[...])
        sums_odd = dot(three_bins(slice(EVEN, ROWS)), w2_odd[...])
        second = []
        for r in range(4):
            here = sums[r * EVEN : (r + 1) * EVEN]
            later = pltpu.roll(here[:, 128:256], EVEN - 1, 0)[:FRAMES]
            total = here[:FRAMES, 0:128] * kept + later + sums_odd[r * FRAMES : (r + 1) * FRAMES]
            second.append(jnp.maximum(total + bias2, 0.0))
        for to in range(SIDE):
            mixed = second[to]
            for r in range(4):
                if r != to:
                    turned = pltpu.roll(second[r], (8 * (r - to)) % 128, 1)
                    mixed = jnp.where(lane_slot == r, turned, mixed)
            maps_out[to, g] = mixed.astype(BF16)
        for dx in (2, 1, 3):
            maps_copy(dx, g).start()
        for step, at in ((0, 0), (1, 4)):
            pl.when(g == at)(lambda step=step: w_step(step))
        return carry

    def maps_sent():
        def step(g, carry):
            for dx in range(1, SIDE):
                maps_copy(dx, g).wait_send()
            return carry

        lax.fori_loop(0, TILES, step, 0)

    drain.append(maps_sent)
    first_odd[4] = jnp.zeros((ROWS, 256), BF16)
    lax.fori_loop(0, TILES, convolve, 0)
    w_step(2)

    for g in range(TILES):
        maps_in[x, g] = maps_out[x, g]

    def maps_wait(g, carry):
        for dx in range(1, SIDE):
            maps_copy(dx, g).wait_recv()
        return carry

    lax.fori_loop(0, TILES, maps_wait, 0)
    for k in range(6):
        w_along_z(k).wait_recv()

    mine = pl.ds(pl.multiple_of(phase * HALF, HALF), HALF)
    theirs = pl.ds(pl.multiple_of(other * HALF, HALF), HALF)

    def sib_copy(n):
        return remote(
            sib_out.at[n], sib_in.at[n], sib_send.at[n], sib_recv.at[n], {"phase": other}
        )

    def rs_copy(dx, n):
        return remote(
            rs_out.at[n, (x + dx) % SIDE],
            rs_in.at[dx - 1, n],
            rs_send.at[dx - 1, n],
            rs_recv.at[dx - 1, n],
            {"seq": row_peer(dx)},
        )

    def project(n):
        cols = pl.ds(pl.multiple_of(n * CUT, CUT), CUT)
        maps = jnp.concatenate(
            [
                jnp.concatenate([maps_in[s, g] for g in range(TILES)], axis=1)
                for s in range(SIDE)
            ],
            axis=0,
        )
        weights = w_all[:, :, cols].reshape(TILES * 128, CUT)
        part[n] = dot(maps, weights).reshape(SIDE, FRAMES, CUT)
        sib_out[n] = part[n, :, theirs, :].astype(BF16)
        sib_copy(n).start()

    def pass_on(n):
        sib_copy(n).wait_recv()
        both = part[n, :, mine, :] + sib_in[n].astype(F32)
        tot[n] = both
        rs_out[n] = both.astype(BF16)
        for dx in (2, 1, 3):
            rs_copy(dx, n).start()

    def project_step(n, carry):
        @pl.when(n < CUTS)
        def _():
            project(n)

        @pl.when(n >= 2)
        def _():
            pass_on(n - 2)

        return carry

    def sums_sent():
        def step(n, carry):
            sib_copy(n).wait_send()
            for dx in range(1, SIDE):
                rs_copy(dx, n).wait_send()
            return carry

        lax.fori_loop(0, CUTS, step, 0)

    drain.append(sums_sent)
    lax.fori_loop(0, CUTS + 2, project_step, 0)

    proj_bias = row_of(pb_ref)
    for n in range(CUTS):
        cols = slice(n * CUT, (n + 1) * CUT)
        for dx in range(1, SIDE):
            rs_copy(dx, n).wait_recv()
        total = tot[n, x]
        for dx in range(1, SIDE):
            total = total + rs_in[dx - 1, n].astype(F32)
        frames_mine[:, cols] = (total + proj_bias[:, cols]).astype(BF16)
    frames_copy = remote(
        frames_mine.at[:, pl.ds(pl.multiple_of(other * LOCAL, LOCAL), LOCAL)],
        frames_cols.at[mine, :],
        fr_send,
        fr_recv,
        {"phase": other},
    )
    frames_copy.start()
    drain.append(frames_copy.wait_send)
    numbers = frames_mine[...].astype(F32)
    average = jnp.mean(numbers, axis=1, keepdims=True)
    centered = numbers - average
    variance = jnp.mean(centered * centered, axis=1, keepdims=True)
    own_slot = pl.ds(pl.multiple_of(REACH * FRAMES + phase * HALF, HALF), HALF)
    normed[own_slot, :] = (centered * lax.rsqrt(variance + 1e-05) * row_of(gain_ref)).astype(BF16)

    def slot(d, k):
        return pl.ds(
            pl.multiple_of((REACH + d) * FRAMES + phase * HALF + k * QUARTER, QUARTER), QUARTER
        )

    def near_copy(d, k):
        step = 1 if d > 0 else -1
        source = normed.at[slot(d - step, k), :]
        target = normed.at[slot(d, k), :]
        sem = (NEAR.index(d), k)
        return remote(source, target, n_send.at[sem], n_recv.at[sem], {"seq": near_peer(-step)})

    def share_copy(d, k):
        rows = normed.at[slot(d, k), :]
        sem = (d + REACH, k)
        return remote(rows, rows, s_send.at[sem], s_recv.at[sem], {"phase": other})

    def near_sent():
        for k in range(2):
            for d in NEAR:
                near_copy(d, k).wait_send()
            for d in range(-REACH, REACH + 1):
                share_copy(d, k).wait_send()

    drain.append(near_sent)
    for k in range(2):
        for d in (-1, 1):
            near_copy(d, k).start()
        share_copy(0, k).start()
    frames_cols[mine, :] = frames_mine[:, pl.ds(pl.multiple_of(phase * LOCAL, LOCAL), LOCAL)]
    qkv_copy.wait()
    out_copy.wait()
    for k in range(2):
        share_copy(0, k).wait_recv()

    def keys_values(low, rows):
        block_rows = normed[low : low + rows, :]
        for n in range(3):
            cols = slice(n * CUT, (n + 1) * CUT)
            keys[low : low + rows, cols] = dot(block_rows, qkv_w[1, :, cols]).astype(BF16)
            values[low : low + rows, cols] = dot(block_rows, qkv_w[2, :, cols]).astype(BF16)

    own_low = REACH * FRAMES
    own_block = normed[own_low : own_low + FRAMES, :]
    for n in range(3):
        cols = slice(n * CUT, (n + 1) * CUT)
        made = dot(own_block, qkv_w[0, :, cols]).astype(BF16)
        query[:, cols] = made * jnp.asarray(1.0 / math.sqrt(HEAD), BF16)
    keys_values(own_low, FRAMES)
    for distance in (1, 2):
        for k in range(2):
            for d in (-distance, distance):
                near_copy(d, k).wait_recv()
                if distance == 1:
                    near_copy(2 * d, k).start()
                share_copy(d, k).start()
        for d in (-distance, distance):
            for k in range(2):
                share_copy(d, k).wait_recv()
            keys_values((REACH + d) * FRAMES, FRAMES)

    lane_low = lax.broadcasted_iota(jnp.int32, (FRAMES, 128), 1) < HEAD

    def attend(pair, carry):
        cols = pl.ds(pl.multiple_of(pair * 128, 128), 128)
        both = query[:, cols]
        zero = jnp.zeros_like(both)
        stacked = jnp.concatenate(
            [jnp.where(lane_low, both, zero), jnp.where(lane_low, zero, both)], axis=0
        )
        scores = lax.dot_general(
            stacked, keys[:, cols], (((1,), (1,)), ((), ())), preferred_element_type=F32
        )
        mask = bias_mask[...]
        scores = scores + jnp.concatenate([mask, mask], axis=0)
        highest = jnp.max(scores, axis=1, keepdims=True)
        weight = jnp.exp(scores - highest)
        denominator = jnp.sum(weight, axis=1, keepdims=True)
        mixed = dot(weight.astype(BF16), values[:, cols]) / denominator
        context[:, cols] = jnp.where(lane_low, mixed[:FRAMES], mixed[FRAMES:]).astype(BF16)
        return carry

    lax.fori_loop(0, LOCAL // 128, attend, 0)

    def br_copy(n):
        return remote(br_out.at[n], br_in.at[n], br_send.at[n], br_recv.at[n], {"phase": other})

    for n in range(3):
        cols = pl.ds(pl.multiple_of(other * LOCAL + n * CUT, CUT), CUT)
        br_out[n] = dot(context[...], out_w[:, cols]).astype(BF16)
        br_copy(n).start()
        drain.append(br_copy(n).wait_send)
    frames_copy.wait_recv()
    for n in range(3):
        cols = pl.ds(pl.multiple_of(phase * LOCAL + n * CUT, CUT), CUT)
        here = slice(n * CUT, (n + 1) * CUT)
        total = frames_cols[:, here].astype(F32) + dot(context[...], out_w[:, cols])
        br_copy(n).wait_recv()
        out_ref[:, here] = (total + br_in[n].astype(F32)).astype(BF16)

    for wait in drain:
        wait()


def local(
    features,
    lengths,
    conv1_weight,
    conv1_bias,
    conv2_weight,
    conv2_bias,
    proj_weight,
    proj_bias,
    norm_gain,
    qkv_weight,
    out_weight,
):
    vmem = pl.BlockSpec(memory_space=pltpu.VMEM)
    smem = pl.BlockSpec(memory_space=pltpu.SMEM)
    hbm = pl.BlockSpec(memory_space=pl.ANY)
    dma = pltpu.SemaphoreType.DMA
    scratch = [
        pltpu.VMEM((4 * FRAMES, 128), BF16),
        pltpu.VMEM((3, 3, 256), F32),
        pltpu.VMEM((2, 128), F32),
        pltpu.VMEM((1, 128), F32),
        pltpu.VMEM((256, WIDTH), BF16),
        pltpu.VMEM((WIDTH // 128, 128), F32),
        pltpu.VMEM((WIDTH // 128, 128), F32),
        pltpu.VMEM((16, 128), BF16),
        pltpu.VMEM((PADDED, 128), F32),
        pltpu.VMEM((384, BINS * 32), BF16),
        pltpu.VMEM((32, 512), F32),
        pltpu.VMEM((4, 128, 512), BF16),
        pltpu.VMEM((TILES, ROWS, 128), BF16),
        pltpu.VMEM((768, 256), BF16),
        pltpu.VMEM((768, 128), BF16),
        pltpu.VMEM((4, ROWS, 256), BF16),
        pltpu.VMEM((5, ROWS, 256), BF16),
        pltpu.VMEM((TILES, 128, WIDTH), BF16),
        pltpu.VMEM((SIDE, TILES, FRAMES, 128), BF16),
        pltpu.VMEM((SIDE, TILES, FRAMES, 128), BF16),
        pltpu.VMEM((CUTS, SIDE, FRAMES, CUT), F32),
        pltpu.VMEM((CUTS, SIDE, HALF, CUT), BF16),
        pltpu.VMEM((CUTS, SIDE, HALF, CUT), BF16),
        pltpu.VMEM((CUTS, SIDE, HALF, CUT), F32),
        pltpu.VMEM((CUTS, SIDE, HALF, CUT), BF16),
        pltpu.VMEM((SIDE - 1, CUTS, HALF, CUT), BF16),
        pltpu.VMEM((HALF, WIDTH), BF16),
        pltpu.VMEM((FRAMES, LOCAL), BF16),
        pltpu.VMEM((SPAN, WIDTH), BF16),
        pltpu.VMEM((3, WIDTH, LOCAL), BF16),
        pltpu.VMEM((LOCAL, WIDTH), BF16),
        pltpu.VMEM((FRAMES, LOCAL), BF16),
        pltpu.VMEM((SPAN, LOCAL), BF16),
        pltpu.VMEM((SPAN, LOCAL), BF16),
        pltpu.VMEM((FRAMES, SPAN), F32),
        pltpu.VMEM((FRAMES, LOCAL), BF16),
        pltpu.VMEM((3, FRAMES, CUT), BF16),
        pltpu.VMEM((3, FRAMES, CUT), BF16),
        dma((7,)),
        dma((9,)),
        dma,
        dma,
        dma,
        dma,
        dma((6,)),
        dma((6,)),
        dma((6,)),
        dma((6,)),
        dma((3, TILES)),
        dma((3, TILES)),
        dma((CUTS,)),
        dma((CUTS,)),
        dma((3, CUTS)),
        dma((3, CUTS)),
        dma,
        dma,
        dma((4, 2)),
        dma((4, 2)),
        dma((5, 2)),
        dma((5, 2)),
        dma((3,)),
        dma((3,)),
    ]
    encoded = pl.pallas_call(
        body,
        out_shape=jax.ShapeDtypeStruct((FRAMES, LOCAL), BF16),
        in_specs=[smem] + [hbm] * 10,
        out_specs=vmem,
        scratch_shapes=scratch,
        compiler_params=pltpu.CompilerParams(
            collective_id=0, has_side_effects=True, vmem_limit_bytes=60 * 1024 * 1024
        ),
    )(
        lengths,
        features[0],
        conv1_weight,
        conv1_bias.reshape(2, 128),
        conv2_weight,
        conv2_bias[None],
        proj_weight,
        proj_bias.reshape(WIDTH // 128, 128),
        norm_gain.reshape(WIDTH // 128, 128),
        qkv_weight.transpose(1, 0, 2),
        out_weight,
    )
    return encoded[None]


def solution(mesh):
    in_specs = (
        P("batch", "seq", None),
        P("batch", None),
        P(),
        P(),
        P(None, None, None, "phase"),
        P("phase"),
        P(("phase", "seq"), None),
        P(),
        P(),
        P(None, None, "phase"),
        P("phase", None),
    )
    out_specs = P("batch", "seq", "phase")
    return jax.shard_map(local, mesh=mesh, in_specs=in_specs, out_specs=out_specs, check_vma=False)
```

```python
import math

import jax
import jax.numpy as jnp
from jax import lax
from jax.experimental import pallas as pl
from jax.experimental.pallas import tpu as pltpu
from jax.sharding import PartitionSpec as P

MESH = pl.DeviceIdType.MESH
BF16 = jnp.bfloat16
F32 = jnp.float32

SIDE = 4
BLOCKS = SIDE * SIDE
FRAMES = 128
HALF = 64
QUARTER = 32
BINS = 32
UTTS = 12
WIDTH = 1536
LOCAL = 768
HEAD = 64
EVEN = 144
ROWS = EVEN + FRAMES
PADDED = 584
TILES = 8
CUT = 256
CUTS = WIDTH // CUT
REACH = 2
SPAN = (2 * REACH + 1) * FRAMES
NEAR = (-2, -1, 1, 2)


def dot(a, b):
    return jnp.dot(a, b, preferred_element_type=F32)


def body(
    lengths_ref,
    feat_hbm,
    w1_hbm,
    b1_hbm,
    w2_ref,
    b2_hbm,
    wp_hbm,
    pb_hbm,
    gain_hbm,
    qkv_ref,
    wo_ref,
    out_ref,
    feat_ref,
    w1_ref,
    b1_ref,
    b2_ref,
    wp_ref,
    pb_ref,
    gain_ref,
    halo,
    padded,
    picker,
    base,
    taps,
    patches,
    w2_even,
    w2_odd,
    even_a,
    odd_a,
    even_b,
    odd_b,
    w_all,
    maps_out,
    maps_in,
    part,
    sib_out,
    sib_in,
    tot,
    rs_out,
    rs_in,
    frames_mine,
    frames_cols,
    normed,
    qkv_w,
    out_w,
    query,
    keys,
    values,
    bias_mask,
    highest_mid,
    denominator_mid,
    numerator_mid,
    context,
    br_out,
    br_in,
    in_sem,
    w2_sem,
    qkv_sem,
    out_sem,
    halo_send,
    halo_recv,
    wy_send,
    wy_recv,
    wz_send,
    wz_recv,
    m_send,
    m_recv,
    sib_send,
    sib_recv,
    rs_send,
    rs_recv,
    fr_send,
    fr_recv,
    n_send,
    n_recv,
    s_send,
    s_recv,
    br_send,
    br_recv,
):
    phase = lax.axis_index("phase")
    block = lax.axis_index("seq")
    x = block % SIDE
    y = block // SIDE
    plane = lax.axis_index("batch")
    planes = lax.axis_size("batch")
    other = 1 - phase

    def row_of(ref):
        return jnp.concatenate([ref[k : k + 1, :] for k in range(WIDTH // 128)], axis=1)

    def row_peer(dx):
        return y * SIDE + (x + dx) % SIDE

    def column_peer(dy):
        return ((y + dy + SIDE) % SIDE) * SIDE + x

    def plane_peer(dz):
        return (plane + dz + planes) % planes

    def near_peer(d):
        return (block + d + BLOCKS) % BLOCKS

    def remote(src, dst, send, recv, target):
        return pltpu.make_async_remote_copy(
            src_ref=src,
            dst_ref=dst,
            send_sem=send,
            recv_sem=recv,
            device_id=target,
            device_id_type=MESH,
        )

    inputs = [
        pltpu.make_async_copy(source, target, in_sem.at[k])
        for k, (source, target) in enumerate(
            (
                (wp_hbm, wp_ref),
                (feat_hbm, feat_ref),
                (w1_hbm, w1_ref),
                (b1_hbm, b1_ref),
                (b2_hbm, b2_ref),
                (pb_hbm, pb_ref),
                (gain_hbm, gain_ref),
            )
        )
    ]
    for copy in inputs:
        copy.start()
    local_w2 = []
    for b in range(3):
        rows = pl.ds(b * 256, 256)
        local_w2.append(
            pltpu.make_async_copy(w2_ref.at[0, b], w2_even.at[rows, pl.ds(0, 128)], w2_sem.at[b])
        )
        local_w2.append(
            pltpu.make_async_copy(
                w2_ref.at[2, b], w2_even.at[rows, pl.ds(128, 128)], w2_sem.at[3 + b]
            )
        )
        local_w2.append(pltpu.make_async_copy(w2_ref.at[1, b], w2_odd.at[rows], w2_sem.at[6 + b]))
    for copy in local_w2:
        copy.start()
    qkv_copy = pltpu.make_async_copy(qkv_ref, qkv_w, qkv_sem)
    out_copy = pltpu.make_async_copy(wo_ref, out_w, out_sem)
    qkv_copy.start()
    out_copy.start()

    barrier = pltpu.get_barrier_semaphore()
    peers = [{"phase": other}]
    peers += [{"seq": row_peer(dx)} for dx in range(1, SIDE)]
    peers += [{"seq": column_peer(dy)} for dy in (1, 3)]
    peers += [{"batch": plane_peer(dz)} for dz in (1, -1)]
    peers += [{"seq": near_peer(d)} for d in (1, -1)]
    for peer in peers:
        pl.semaphore_signal(barrier, inc=1, device_id=peer, device_id_type=MESH)

    out_row = lax.broadcasted_iota(jnp.int32, (256, 256), 0)
    in_row = lax.broadcasted_iota(jnp.int32, (256, 256), 1)
    reorder = jnp.where(in_row == (out_row & 7) * BINS + (out_row >> 3), 1.0, 0.0).astype(BF16)
    own_rows = pl.ds(pl.multiple_of(y * 32, 32), 32)
    inputs[0].wait()
    for n in range(CUTS):
        cols = slice(n * CUT, (n + 1) * CUT)
        moved = dot(reorder, wp_ref[:, cols]).astype(BF16)
        for g in range(TILES):
            w_all[g, own_rows, cols] = moved[g * 32 : (g + 1) * 32]

    inputs[1].wait()
    pl.semaphore_wait(barrier, len(peers))

    halo_copy = remote(
        feat_ref.at[pl.ds(496, 16)], halo, halo_send, halo_recv, {"seq": near_peer(1)}
    )
    halo_copy.start()
    drain = [halo_copy.wait_send]
    half_low = (plane % 2) * 4
    pieces = [
        (-1, 0, 1),
        (1, 1, -1),
        (-1, 1, -1),
        (1, 0, 1),
        (2, 0, 1),
        (2, 1, -1),
    ]

    def w_piece(dy, part_of, low):
        rows = pl.ds(pl.multiple_of(((y + dy + SIDE) % SIDE) * 32, 32), 32)
        return w_all.at[pl.ds(low + 2 * part_of, 2), rows, :]

    def w_along_y(k):
        dy, part_of, _ = pieces[k]
        step = -1 if dy == -1 or (dy == 2 and part_of == 0) else 1
        mine = w_piece(dy - step, part_of, half_low)
        return remote(
            mine, mine, wy_send.at[k], wy_recv.at[k], {"seq": column_peer(-step)}
        )

    def w_along_z(k):
        dy, part_of, dz = pieces[k]
        mine = w_piece(dy, part_of, half_low)
        return remote(mine, mine, wz_send.at[k], wz_recv.at[k], {"batch": plane_peer(dz)})

    def w_sent():
        for k in range(6):
            w_along_y(k).wait_send()
            w_along_z(k).wait_send()

    drain.append(w_sent)
    for k in range(4):
        w_along_y(k).start()

    def w_step(step):
        for k in (2 * step, 2 * step + 1):
            w_along_y(k).wait_recv()
            if step == 0:
                w_along_y(4 + k).start()
            w_along_z(k).start()

    offsets = []
    running = jnp.int32(0)
    for i in range(UTTS):
        offsets.append(running)
        running = running + lengths_ref[0, i]
    place = lax.broadcasted_iota(jnp.int32, (FRAMES, 128), 0) + block * FRAMES
    starts = place == offsets[0]
    seg_query = jnp.where(place >= offsets[0], 1, 0)
    for off in offsets[1:]:
        starts = starts | (place == off)
        seg_query = seg_query + jnp.where(place >= off, 1, 0)
    kept = jnp.where(starts, 0.0, 1.0)
    key_place = lax.broadcasted_iota(jnp.int32, (8, SPAN), 1) + (block - REACH) * FRAMES
    seg_key = jnp.where(key_place >= offsets[0], 1, 0)
    for off in offsets[1:]:
        seg_key = seg_key + jnp.where(key_place >= off, 1, 0)
    seg_key = jnp.where((key_place >= 0) & (key_place < BLOCKS * FRAMES), seg_key, 0)
    for j in range(SPAN // 128):
        cols = slice(j * 128, (j + 1) * 128)
        bias_mask[:, cols] = jnp.where(seg_query == seg_key[0:1, cols], 0.0, -1e30)

    for copy in inputs[2:]:
        copy.wait()
    base[...] = jnp.zeros_like(base)

    def two_pieces(value):
        high = value.astype(BF16).astype(F32)
        return high, value - high

    for a in range(3):
        pair = two_pieces(w1_ref[a])
        for b in range(3):
            for shift in range(2):
                for k in range(2):
                    row = 15 * k + 5 * a + 2 * shift + b
                    base[row : row + 1, shift * 256 : (shift + 1) * 256] = pair[k][b : b + 1, :]
    pair = two_pieces(jnp.concatenate([b1_ref[0:1, :], b1_ref[1:2, :]], axis=1))
    for k in range(2):
        for shift in range(2):
            base[30 + k : 31 + k, shift * 256 : (shift + 1) * 256] = pair[k]
    taps[...] = jnp.zeros_like(taps)
    for r in range(4):
        taps[r, 32 * r : 32 * r + 32, :] = base[...].astype(BF16)

    lane = lax.broadcasted_iota(jnp.int32, (1, BINS * 32), 1)
    low = lane & 31
    tap = jnp.where(low >= 15, low - 15, low)
    tap_time = jnp.where(tap >= 5, 1, 0) + jnp.where(tap >= 10, 1, 0)
    tap_bin = (lane >> 5) * 4 + (tap - 5 * tap_time) - 1
    wanted = jnp.where((low < 30) & (tap_bin >= 0), tap_time * 128 + tap_bin, -1)
    constant = jnp.where(low >= 30, 1.0, 0.0)
    for a in range(3):
        bins_in = lax.broadcasted_iota(jnp.int32, (128, BINS * 32), 0) + a * 128
        picker[a * 128 : (a + 1) * 128, :] = jnp.where(bins_in == wanted, 1.0, 0.0).astype(BF16)

    padded[8:520, :] = feat_ref[...].astype(F32)
    padded[520:PADDED, :] = jnp.zeros((PADDED - 520, 128), F32)
    halo_copy.wait_recv()
    first = jnp.where(block > 0, 1.0, 0.0)
    padded[0:8, :] = halo[...].astype(F32)[8:16] * first
    even = [padded[pl.ds(5 + a, EVEN, stride=4), :] for a in range(3)]
    odd = [padded[pl.ds(7 + a, FRAMES, stride=4), :] for a in range(3)]
    odd[0] = odd[0] * kept
    gathered = jnp.concatenate(
        [jnp.concatenate(even, axis=1), jnp.concatenate(odd, axis=1)], axis=0
    ).astype(BF16)
    for k in range(4):
        cols = slice(k * 256, (k + 1) * 256)
        made = (dot(gathered, picker[:, cols]) + constant[:, cols]).astype(BF16)
        patches[2 * k] = made[:, 0:128]
        patches[2 * k + 1] = made[:, 128:256]

    for copy in local_w2:
        copy.wait()

    lane_slot = (lax.broadcasted_iota(jnp.int32, (FRAMES, 128), 1) >> 3) & 3
    bias2 = b2_ref[...]

    def maps_copy(dx, g):
        return remote(
            maps_out.at[(x + dx) % SIDE, g],
            maps_in.at[x, g],
            m_send.at[dx - 1, g],
            m_recv.at[dx - 1, g],
            {"seq": row_peer(dx)},
        )

    def first_convolution(g, evens, odds, last_odds):
        patch = patches[g]
        odds[0] = last_odds[4]
        for r in range(4):
            evens[r] = jnp.maximum(dot(patch, taps[r, :, 0:256]), 0.0).astype(BF16)
            odds[r + 1] = jnp.maximum(dot(patch, taps[r, :, 256:512]), 0.0).astype(BF16)

    def second_convolution(g, evens, odds):
        def three_bins(rows):
            return jnp.concatenate(
                [
                    jnp.concatenate([odds[r, rows], evens[r, rows], odds[r + 1, rows]], axis=1)
                    for r in range(4)
                ],
                axis=0,
            )

        sums = dot(three_bins(slice(0, EVEN)), w2_even[...])
        sums_odd = dot(three_bins(slice(EVEN, ROWS)), w2_odd[...])
        second = []
        for r in range(4):
            here = sums[r * EVEN : (r + 1) * EVEN]
            later = pltpu.roll(here[:, 128:256], EVEN - 1, 0)[:FRAMES]
            total = here[:FRAMES, 0:128] * kept + later + sums_odd[r * FRAMES : (r + 1) * FRAMES]
            second.append(jnp.maximum(total + bias2, 0.0))
        for to in range(SIDE):
            mixed = second[to]
            for r in range(4):
                if r != to:
                    turned = pltpu.roll(second[r], (8 * (r - to)) % 128, 1)
                    mixed = jnp.where(lane_slot == r, turned, mixed)
            maps_out[to, g] = mixed.astype(BF16)
        for dx in (2, 1, 3):
            maps_copy(dx, g).start()

    def convolve(pair, carry):
        g = 2 * pair
        first_convolution(g + 1, even_b, odd_b, odd_a)
        second_convolution(g, even_a, odd_a)
        first_convolution(g + 2, even_a, odd_a, odd_b)
        second_convolution(g + 1, even_b, odd_b)
        for step, at in ((1, 0), (2, 2)):
            pl.when(pair == at)(lambda step=step: w_step(step))
        return carry

    def maps_sent():
        def step(g, carry):
            for dx in range(1, SIDE):
                maps_copy(dx, g).wait_send()
            return carry

        lax.fori_loop(0, TILES, step, 0)

    drain.append(maps_sent)
    odd_b[4] = jnp.zeros((ROWS, 256), BF16)
    first_convolution(0, even_a, odd_a, odd_b)
    w_step(0)
    lax.fori_loop(0, TILES // 2 - 1, convolve, 0)
    first_convolution(TILES - 1, even_b, odd_b, odd_a)
    second_convolution(TILES - 2, even_a, odd_a)
    second_convolution(TILES - 1, even_b, odd_b)

    for g in range(TILES):
        maps_in[x, g] = maps_out[x, g]

    def maps_wait(g, carry):
        for dx in range(1, SIDE):
            maps_copy(dx, g).wait_recv()
        return carry

    lax.fori_loop(0, TILES, maps_wait, 0)
    mine = pl.ds(pl.multiple_of(phase * HALF, HALF), HALF)
    theirs = pl.ds(pl.multiple_of(other * HALF, HALF), HALF)

    def sib_copy(n):
        return remote(
            sib_out.at[n], sib_in.at[n], sib_send.at[n], sib_recv.at[n], {"phase": other}
        )

    def rs_copy(dx, n):
        return remote(
            rs_out.at[n, (x + dx) % SIDE],
            rs_in.at[dx - 1, n],
            rs_send.at[dx - 1, n],
            rs_recv.at[dx - 1, n],
            {"seq": row_peer(dx)},
        )

    def half_sums(n, low):
        cols = pl.ds(pl.multiple_of(n * CUT, CUT), CUT)
        maps = jnp.concatenate(
            [
                jnp.concatenate([maps_in[s, low + g] for g in range(4)], axis=1)
                for s in range(SIDE)
            ],
            axis=0,
        )
        weights = w_all[pl.ds(low, 4), :, cols].reshape(4 * 128, CUT)
        return dot(maps, weights).reshape(SIDE, FRAMES, CUT)

    def early(n, carry):
        part[n] = half_sums(n, half_low)
        return carry

    lax.fori_loop(0, CUTS, early, 0)
    for k in range(6):
        w_along_z(k).wait_recv()

    def project(n):
        part[n] += half_sums(n, 4 - half_low)
        sib_out[n] = part[n, :, theirs, :].astype(BF16)
        sib_copy(n).start()

    def pass_on(n):
        sib_copy(n).wait_recv()
        both = part[n, :, mine, :] + sib_in[n].astype(F32)
        tot[n] = both
        rs_out[n] = both.astype(BF16)
        for dx in (2, 1, 3):
            rs_copy(dx, n).start()

    def project_step(n, carry):
        @pl.when(n < CUTS)
        def _():
            project(n)

        @pl.when(n >= 2)
        def _():
            pass_on(n - 2)

        return carry

    def sums_sent():
        def step(n, carry):
            sib_copy(n).wait_send()
            for dx in range(1, SIDE):
                rs_copy(dx, n).wait_send()
            return carry

        lax.fori_loop(0, CUTS, step, 0)

    drain.append(sums_sent)
    lax.fori_loop(0, CUTS + 2, project_step, 0)

    proj_bias = row_of(pb_ref)
    for n in range(CUTS):
        cols = slice(n * CUT, (n + 1) * CUT)
        for dx in range(1, SIDE):
            rs_copy(dx, n).wait_recv()
        total = tot[n, x]
        for dx in range(1, SIDE):
            total = total + rs_in[dx - 1, n].astype(F32)
        frames_mine[:, cols] = (total + proj_bias[:, cols]).astype(BF16)
    frames_copy = remote(
        frames_mine.at[:, pl.ds(pl.multiple_of(other * LOCAL, LOCAL), LOCAL)],
        frames_cols.at[mine, :],
        fr_send,
        fr_recv,
        {"phase": other},
    )
    frames_copy.start()
    drain.append(frames_copy.wait_send)
    numbers = frames_mine[...].astype(F32)
    average = jnp.mean(numbers, axis=1, keepdims=True)
    centered = numbers - average
    variance = jnp.mean(centered * centered, axis=1, keepdims=True)
    own_slot = pl.ds(pl.multiple_of(REACH * FRAMES + phase * HALF, HALF), HALF)
    normed[own_slot, :] = (centered * lax.rsqrt(variance + 1e-05) * row_of(gain_ref)).astype(BF16)

    def slot(d, k):
        return pl.ds(
            pl.multiple_of((REACH + d) * FRAMES + phase * HALF + k * QUARTER, QUARTER), QUARTER
        )

    def near_copy(d, k):
        step = 1 if d > 0 else -1
        source = normed.at[slot(d - step, k), :]
        target = normed.at[slot(d, k), :]
        sem = (NEAR.index(d), k)
        return remote(source, target, n_send.at[sem], n_recv.at[sem], {"seq": near_peer(-step)})

    def share_copy(d, k):
        rows = normed.at[slot(d, k), :]
        sem = (d + REACH, k)
        return remote(rows, rows, s_send.at[sem], s_recv.at[sem], {"phase": other})

    def near_sent():
        for k in range(2):
            for d in NEAR:
                near_copy(d, k).wait_send()
            for d in range(-REACH, REACH + 1):
                share_copy(d, k).wait_send()

    drain.append(near_sent)
    for k in range(2):
        for d in (-1, 1):
            near_copy(d, k).start()
        share_copy(0, k).start()
    frames_cols[mine, :] = frames_mine[:, pl.ds(pl.multiple_of(phase * LOCAL, LOCAL), LOCAL)]
    qkv_copy.wait()
    out_copy.wait()
    for k in range(2):
        share_copy(0, k).wait_recv()

    def keys_values(lows):
        block_rows = jnp.concatenate([normed[low : low + FRAMES, :] for low in lows], axis=0)
        for n in range(3):
            cols = slice(n * CUT, (n + 1) * CUT)
            for j, target in ((1, keys), (2, values)):
                made = dot(block_rows, qkv_w[j, :, cols]).astype(BF16)
                for i, low in enumerate(lows):
                    target[low : low + FRAMES, cols] = made[i * FRAMES : (i + 1) * FRAMES]

    own_low = REACH * FRAMES
    own_block = normed[own_low : own_low + FRAMES, :]
    for n in range(3):
        cols = slice(n * CUT, (n + 1) * CUT)
        made = dot(own_block, qkv_w[0, :, cols]).astype(BF16)
        query[:, cols] = made * jnp.asarray(1.0 / math.sqrt(HEAD), BF16)
    keys_values([own_low])
    lane_low = lax.broadcasted_iota(jnp.int32, (FRAMES, 128), 1) < HEAD

    def pair_scores(pair, pieces_of):
        cols = pl.ds(pl.multiple_of(pair * 128, 128), 128)
        both = query[:, cols]
        zero = jnp.zeros_like(both)
        stacked = jnp.concatenate(
            [jnp.where(lane_low, both, zero), jnp.where(lane_low, zero, both)], axis=0
        )
        near_keys = jnp.concatenate([keys[rows, cols] for rows in pieces_of], axis=0)
        near_values = jnp.concatenate([values[rows, cols] for rows in pieces_of], axis=0)
        mask = jnp.concatenate([bias_mask[:, rows] for rows in pieces_of], axis=1)
        scores = lax.dot_general(
            stacked, near_keys, (((1,), (1,)), ((), ())), preferred_element_type=F32
        )
        return scores + jnp.concatenate([mask, mask], axis=0), near_values

    middle = [slice(FRAMES, 4 * FRAMES)]
    far = [slice(0, FRAMES), slice(4 * FRAMES, 5 * FRAMES)]

    def attend_middle(pair, carry):
        scores, near_values = pair_scores(pair, middle)
        highest = jnp.max(scores, axis=1, keepdims=True)
        weight = jnp.exp(scores - highest)
        highest_mid[pair] = jnp.broadcast_to(highest, (2 * FRAMES, 128))
        denominator = jnp.sum(weight, axis=1, keepdims=True)
        denominator_mid[pair] = jnp.broadcast_to(denominator, (2 * FRAMES, 128))
        numerator_mid[pair] = dot(weight.astype(BF16), near_values)
        return carry

    def attend_far(pair, carry):
        scores, near_values = pair_scores(pair, far)
        before = highest_mid[pair]
        highest = jnp.maximum(before, jnp.max(scores, axis=1, keepdims=True))
        factor = jnp.exp(before - highest)
        weight = jnp.exp(scores - jnp.concatenate([highest, highest], axis=1))
        denominator = denominator_mid[pair] * factor + jnp.sum(weight, axis=1, keepdims=True)
        numerator = numerator_mid[pair] * factor + dot(weight.astype(BF16), near_values)
        mixed = numerator / denominator
        cols = pl.ds(pl.multiple_of(pair * 128, 128), 128)
        context[:, cols] = jnp.where(lane_low, mixed[:FRAMES], mixed[FRAMES:]).astype(BF16)
        return carry

    for k in range(2):
        for d in (-1, 1):
            near_copy(d, k).wait_recv()
            near_copy(2 * d, k).start()
            share_copy(d, k).start()
    for k in range(2):
        for d in (-1, 1):
            share_copy(d, k).wait_recv()
    keys_values([FRAMES, 3 * FRAMES])
    lax.fori_loop(0, LOCAL // 128, attend_middle, 0)
    for k in range(2):
        for d in (-2, 2):
            near_copy(d, k).wait_recv()
            share_copy(d, k).start()
    for k in range(2):
        for d in (-2, 2):
            share_copy(d, k).wait_recv()
    keys_values([0, 4 * FRAMES])
    lax.fori_loop(0, LOCAL // 128, attend_far, 0)

    def br_copy(n):
        return remote(br_out.at[n], br_in.at[n], br_send.at[n], br_recv.at[n], {"phase": other})

    for n in range(3):
        cols = pl.ds(pl.multiple_of(other * LOCAL + n * CUT, CUT), CUT)
        br_out[n] = dot(context[...], out_w[:, cols]).astype(BF16)
        br_copy(n).start()
        drain.append(br_copy(n).wait_send)
    frames_copy.wait_recv()
    for n in range(3):
        cols = pl.ds(pl.multiple_of(phase * LOCAL + n * CUT, CUT), CUT)
        here = slice(n * CUT, (n + 1) * CUT)
        total = frames_cols[:, here].astype(F32) + dot(context[...], out_w[:, cols])
        br_copy(n).wait_recv()
        out_ref[:, here] = (total + br_in[n].astype(F32)).astype(BF16)

    for wait in drain:
        wait()


def local(
    features,
    lengths,
    conv1_weight,
    conv1_bias,
    conv2_weight,
    conv2_bias,
    proj_weight,
    proj_bias,
    norm_gain,
    qkv_weight,
    out_weight,
):
    vmem = pl.BlockSpec(memory_space=pltpu.VMEM)
    smem = pl.BlockSpec(memory_space=pltpu.SMEM)
    hbm = pl.BlockSpec(memory_space=pl.ANY)
    dma = pltpu.SemaphoreType.DMA
    scratch = [
        pltpu.VMEM((4 * FRAMES, 128), BF16),
        pltpu.VMEM((3, 3, 256), F32),
        pltpu.VMEM((2, 128), F32),
        pltpu.VMEM((1, 128), F32),
        pltpu.VMEM((256, WIDTH), BF16),
        pltpu.VMEM((WIDTH // 128, 128), F32),
        pltpu.VMEM((WIDTH // 128, 128), F32),
        pltpu.VMEM((16, 128), BF16),
        pltpu.VMEM((PADDED, 128), F32),
        pltpu.VMEM((384, BINS * 32), BF16),
        pltpu.VMEM((32, 512), F32),
        pltpu.VMEM((4, 128, 512), BF16),
        pltpu.VMEM((TILES, ROWS, 128), BF16),
        pltpu.VMEM((768, 256), BF16),
        pltpu.VMEM((768, 128), BF16),
        pltpu.VMEM((4, ROWS, 256), BF16),
        pltpu.VMEM((5, ROWS, 256), BF16),
        pltpu.VMEM((4, ROWS, 256), BF16),
        pltpu.VMEM((5, ROWS, 256), BF16),
        pltpu.VMEM((TILES, 128, WIDTH), BF16),
        pltpu.VMEM((SIDE, TILES, FRAMES, 128), BF16),
        pltpu.VMEM((SIDE, TILES, FRAMES, 128), BF16),
        pltpu.VMEM((CUTS, SIDE, FRAMES, CUT), F32),
        pltpu.VMEM((CUTS, SIDE, HALF, CUT), BF16),
        pltpu.VMEM((CUTS, SIDE, HALF, CUT), BF16),
        pltpu.VMEM((CUTS, SIDE, HALF, CUT), F32),
        pltpu.VMEM((CUTS, SIDE, HALF, CUT), BF16),
        pltpu.VMEM((SIDE - 1, CUTS, HALF, CUT), BF16),
        pltpu.VMEM((HALF, WIDTH), BF16),
        pltpu.VMEM((FRAMES, LOCAL), BF16),
        pltpu.VMEM((SPAN, WIDTH), BF16),
        pltpu.VMEM((3, WIDTH, LOCAL), BF16),
        pltpu.VMEM((LOCAL, WIDTH), BF16),
        pltpu.VMEM((FRAMES, LOCAL), BF16),
        pltpu.VMEM((SPAN, LOCAL), BF16),
        pltpu.VMEM((SPAN, LOCAL), BF16),
        pltpu.VMEM((FRAMES, SPAN), F32),
        pltpu.VMEM((6, 2 * FRAMES, 128), F32),
        pltpu.VMEM((6, 2 * FRAMES, 128), F32),
        pltpu.VMEM((6, 2 * FRAMES, 128), F32),
        pltpu.VMEM((FRAMES, LOCAL), BF16),
        pltpu.VMEM((3, FRAMES, CUT), BF16),
        pltpu.VMEM((3, FRAMES, CUT), BF16),
        dma((7,)),
        dma((9,)),
        dma,
        dma,
        dma,
        dma,
        dma((6,)),
        dma((6,)),
        dma((6,)),
        dma((6,)),
        dma((3, TILES)),
        dma((3, TILES)),
        dma((CUTS,)),
        dma((CUTS,)),
        dma((3, CUTS)),
        dma((3, CUTS)),
        dma,
        dma,
        dma((4, 2)),
        dma((4, 2)),
        dma((5, 2)),
        dma((5, 2)),
        dma((3,)),
        dma((3,)),
    ]
    encoded = pl.pallas_call(
        body,
        out_shape=jax.ShapeDtypeStruct((FRAMES, LOCAL), BF16),
        in_specs=[smem] + [hbm] * 10,
        out_specs=vmem,
        scratch_shapes=scratch,
        compiler_params=pltpu.CompilerParams(
            collective_id=0, has_side_effects=True, vmem_limit_bytes=60 * 1024 * 1024
        ),
    )(
        lengths,
        features[0],
        conv1_weight,
        conv1_bias.reshape(2, 128),
        conv2_weight,
        conv2_bias[None],
        proj_weight,
        proj_bias.reshape(WIDTH // 128, 128),
        norm_gain.reshape(WIDTH // 128, 128),
        qkv_weight.transpose(1, 0, 2),
        out_weight,
    )
    return encoded[None]


def solution(mesh):
    in_specs = (
        P("batch", "seq", None),
        P("batch", None),
        P(),
        P(),
        P(None, None, None, "phase"),
        P("phase"),
        P(("phase", "seq"), None),
        P(),
        P(),
        P(None, None, "phase"),
        P("phase", None),
    )
    out_specs = P("batch", "seq", "phase")
    return jax.shard_map(local, mesh=mesh, in_specs=in_specs, out_specs=out_specs, check_vma=False)
```

```python
import math

import jax
import jax.numpy as jnp
from jax import lax
from jax.experimental import pallas as pl
from jax.experimental.pallas import tpu as pltpu
from jax.sharding import PartitionSpec as P

MESH = pl.DeviceIdType.MESH
BF16 = jnp.bfloat16
F32 = jnp.float32

SIDE = 4
BLOCKS = SIDE * SIDE
FRAMES = 128
HALF = 64
QUARTER = 32
BINS = 32
UTTS = 12
WIDTH = 1536
LOCAL = 768
HEAD = 64
EVEN = 144
ROWS = EVEN + FRAMES
PADDED = 584
TILES = 8
CUT = 256
CUTS = WIDTH // CUT
REACH = 2
SPAN = (2 * REACH + 1) * FRAMES
NEAR = (-2, -1, 1, 2)


def dot(a, b):
    return jnp.dot(a, b, preferred_element_type=F32)


def body(
    lengths_ref,
    feat_hbm,
    w1_hbm,
    b1_hbm,
    w2_ref,
    b2_hbm,
    wp_hbm,
    pb_hbm,
    gain_hbm,
    qkv_ref,
    wo_ref,
    out_ref,
    feat_ref,
    w1_ref,
    b1_ref,
    b2_ref,
    wp_ref,
    pb_ref,
    gain_ref,
    halo,
    padded,
    picker,
    base,
    taps,
    patches,
    w2_even,
    w2_odd,
    first_even,
    first_odd,
    w_all,
    maps_out,
    maps_in,
    part,
    sib_out,
    sib_in,
    tot,
    rs_out,
    rs_in,
    frames_mine,
    frames_cols,
    normed,
    qkv_w,
    out_w,
    query,
    keys,
    values,
    bias_mask,
    context,
    br_out,
    br_in,
    in_sem,
    w2_sem,
    qkv_sem,
    out_sem,
    halo_send,
    halo_recv,
    wy_send,
    wy_recv,
    wz_send,
    wz_recv,
    m_send,
    m_recv,
    sib_send,
    sib_recv,
    rs_send,
    rs_recv,
    fr_send,
    fr_recv,
    n_send,
    n_recv,
    s_send,
    s_recv,
    br_send,
    br_recv,
):
    phase = lax.axis_index("phase")
    block = lax.axis_index("seq")
    x = block % SIDE
    y = block // SIDE
    plane = lax.axis_index("batch")
    partner = plane + 1 - 2 * (plane % 2)
    other = 1 - phase

    def row_of(ref):
        return jnp.concatenate([ref[k : k + 1, :] for k in range(WIDTH // 128)], axis=1)

    def row_peer(dx):
        return y * SIDE + (x + dx) % SIDE

    def column_peer(dy):
        return ((y + dy + SIDE) % SIDE) * SIDE + x

    def near_peer(d):
        return (block + d + BLOCKS) % BLOCKS

    def remote(src, dst, send, recv, target):
        return pltpu.make_async_remote_copy(
            src_ref=src,
            dst_ref=dst,
            send_sem=send,
            recv_sem=recv,
            device_id=target,
            device_id_type=MESH,
        )

    inputs = [
        pltpu.make_async_copy(source, target, in_sem.at[k])
        for k, (source, target) in enumerate(
            (
                (wp_hbm, wp_ref),
                (feat_hbm, feat_ref),
                (w1_hbm, w1_ref),
                (b1_hbm, b1_ref),
                (b2_hbm, b2_ref),
                (pb_hbm, pb_ref),
                (gain_hbm, gain_ref),
            )
        )
    ]
    for copy in inputs:
        copy.start()
    local_w2 = []
    for b in range(3):
        rows = pl.ds(b * 256, 256)
        local_w2.append(
            pltpu.make_async_copy(w2_ref.at[0, b], w2_even.at[rows, pl.ds(0, 128)], w2_sem.at[b])
        )
        local_w2.append(
            pltpu.make_async_copy(
                w2_ref.at[2, b], w2_even.at[rows, pl.ds(128, 128)], w2_sem.at[3 + b]
            )
        )
        local_w2.append(pltpu.make_async_copy(w2_ref.at[1, b], w2_odd.at[rows], w2_sem.at[6 + b]))
    for copy in local_w2:
        copy.start()
    qkv_copy = pltpu.make_async_copy(qkv_ref, qkv_w, qkv_sem)
    out_copy = pltpu.make_async_copy(wo_ref, out_w, out_sem)
    qkv_copy.start()
    out_copy.start()

    barrier = pltpu.get_barrier_semaphore()
    peers = [{"phase": other}]
    peers += [{"seq": row_peer(dx)} for dx in range(1, SIDE)]
    peers += [{"seq": column_peer(dy)} for dy in (1, 3)]
    peers += [{"batch": partner}]
    peers += [{"seq": near_peer(d)} for d in (1, -1)]
    for peer in peers:
        pl.semaphore_signal(barrier, inc=1, device_id=peer, device_id_type=MESH)

    out_row = lax.broadcasted_iota(jnp.int32, (256, 256), 0)
    in_row = lax.broadcasted_iota(jnp.int32, (256, 256), 1)
    reorder = jnp.where(in_row == (out_row & 7) * BINS + (out_row >> 3), 1.0, 0.0).astype(BF16)
    own_rows = pl.ds(pl.multiple_of(y * 32, 32), 32)
    inputs[0].wait()
    for n in range(CUTS):
        cols = slice(n * CUT, (n + 1) * CUT)
        moved = dot(reorder, wp_ref[:, cols]).astype(BF16)
        for g in range(TILES):
            w_all[g, own_rows, cols] = moved[g * 32 : (g + 1) * 32]

    inputs[1].wait()
    pl.semaphore_wait(barrier, len(peers))

    halo_copy = remote(
        feat_ref.at[pl.ds(496, 16)], halo, halo_send, halo_recv, {"seq": near_peer(1)}
    )
    halo_copy.start()
    drain = [halo_copy.wait_send]
    own_groups = 2 * (plane % 2)
    along_y = [
        (-1, own_groups, 2, -1),
        (1, own_groups, 2, 1),
        (-1, 4, 2, -1),
        (1, 6, 2, 1),
        (-1, 6, 2, -1),
        (1, 4, 2, 1),
        (2, own_groups, 1, -1),
        (2, own_groups + 1, 1, 1),
        (2, 4, 2, -1),
        (2, 6, 2, 1),
    ]
    along_z = [
        (-1, own_groups, 2),
        (1, own_groups, 2),
        (2, own_groups, 1),
        (2, own_groups + 1, 1),
    ]

    def w_piece(dy, low, groups):
        rows = pl.ds(pl.multiple_of(((y + dy + SIDE) % SIDE) * 32, 32), 32)
        return w_all.at[pl.ds(low, groups), rows, :]

    def w_along_y(k):
        dy, low, groups, side = along_y[k]
        piece = w_piece(dy - side, low, groups)
        return remote(piece, piece, wy_send.at[k], wy_recv.at[k], {"seq": column_peer(-side)})

    def w_along_z(k):
        piece = w_piece(*along_z[k])
        return remote(piece, piece, wz_send.at[k], wz_recv.at[k], {"batch": partner})

    def w_sent():
        for k in range(10):
            w_along_y(k).wait_send()
        for k in range(4):
            w_along_z(k).wait_send()

    drain.append(w_sent)
    for k in range(4):
        w_along_y(k).start()

    def w_step(step):
        if step == 0:
            for k in (0, 1):
                w_along_y(k).wait_recv()
                w_along_y(6 + k).start()
                w_along_z(k).start()
            for k in (4, 5):
                w_along_y(k).start()
        if step == 1:
            for k in (2, 3):
                w_along_y(k).wait_recv()
                w_along_y(6 + k).start()
        if step == 2:
            for k in (6, 7):
                w_along_y(k).wait_recv()
                w_along_z(k - 4).start()

    offsets = []
    running = jnp.int32(0)
    for i in range(UTTS):
        offsets.append(running)
        running = running + lengths_ref[0, i]
    place = lax.broadcasted_iota(jnp.int32, (FRAMES, 128), 0) + block * FRAMES
    starts = place == offsets[0]
    seg_query = jnp.where(place >= offsets[0], 1, 0)
    for off in offsets[1:]:
        starts = starts | (place == off)
        seg_query = seg_query + jnp.where(place >= off, 1, 0)
    kept = jnp.where(starts, 0.0, 1.0)
    key_place = lax.broadcasted_iota(jnp.int32, (8, SPAN), 1) + (block - REACH) * FRAMES
    seg_key = jnp.where(key_place >= offsets[0], 1, 0)
    for off in offsets[1:]:
        seg_key = seg_key + jnp.where(key_place >= off, 1, 0)
    seg_key = jnp.where((key_place >= 0) & (key_place < BLOCKS * FRAMES), seg_key, 0)
    for j in range(SPAN // 128):
        cols = slice(j * 128, (j + 1) * 128)
        bias_mask[:, cols] = jnp.where(seg_query == seg_key[0:1, cols], 0.0, -1e30)

    for copy in inputs[2:]:
        copy.wait()
    base[...] = jnp.zeros_like(base)

    def two_pieces(value):
        high = value.astype(BF16).astype(F32)
        return high, value - high

    for a in range(3):
        pair = two_pieces(w1_ref[a])
        for b in range(3):
            for shift in range(2):
                for k in range(2):
                    row = 15 * k + 5 * a + 2 * shift + b
                    base[row : row + 1, shift * 256 : (shift + 1) * 256] = pair[k][b : b + 1, :]
    pair = two_pieces(jnp.concatenate([b1_ref[0:1, :], b1_ref[1:2, :]], axis=1))
    for k in range(2):
        for shift in range(2):
            base[30 + k : 31 + k, shift * 256 : (shift + 1) * 256] = pair[k]
    taps[...] = jnp.zeros_like(taps)
    for r in range(4):
        taps[r, 32 * r : 32 * r + 32, :] = base[...].astype(BF16)

    lane = lax.broadcasted_iota(jnp.int32, (1, BINS * 32), 1)
    low = lane & 31
    tap = jnp.where(low >= 15, low - 15, low)
    tap_time = jnp.where(tap >= 5, 1, 0) + jnp.where(tap >= 10, 1, 0)
    tap_bin = (lane >> 5) * 4 + (tap - 5 * tap_time) - 1
    wanted = jnp.where((low < 30) & (tap_bin >= 0), tap_time * 128 + tap_bin, -1)
    constant = jnp.where(low >= 30, 1.0, 0.0)
    for a in range(3):
        bins_in = lax.broadcasted_iota(jnp.int32, (128, BINS * 32), 0) + a * 128
        picker[a * 128 : (a + 1) * 128, :] = jnp.where(bins_in == wanted, 1.0, 0.0).astype(BF16)

    padded[8:520, :] = feat_ref[...].astype(F32)
    padded[520:PADDED, :] = jnp.zeros((PADDED - 520, 128), F32)
    halo_copy.wait_recv()
    first = jnp.where(block > 0, 1.0, 0.0)
    padded[0:8, :] = halo[...].astype(F32)[8:16] * first
    even = [padded[pl.ds(5 + a, EVEN, stride=4), :] for a in range(3)]
    odd = [padded[pl.ds(7 + a, FRAMES, stride=4), :] for a in range(3)]
    odd[0] = odd[0] * kept
    gathered = jnp.concatenate(
        [jnp.concatenate(even, axis=1), jnp.concatenate(odd, axis=1)], axis=0
    ).astype(BF16)
    for k in range(4):
        cols = slice(k * 256, (k + 1) * 256)
        made = (dot(gathered, picker[:, cols]) + constant[:, cols]).astype(BF16)
        patches[2 * k] = made[:, 0:128]
        patches[2 * k + 1] = made[:, 128:256]

    for copy in local_w2:
        copy.wait()

    lane_slot = (lax.broadcasted_iota(jnp.int32, (FRAMES, 128), 1) >> 3) & 3
    bias2 = b2_ref[...]

    def maps_copy(dx, g):
        return remote(
            maps_out.at[(x + dx) % SIDE, g],
            maps_in.at[x, g],
            m_send.at[dx - 1, g],
            m_recv.at[dx - 1, g],
            {"seq": row_peer(dx)},
        )

    def convolve(g, carry):
        patch = patches[g]
        first_odd[0] = first_odd[4]
        for r in range(4):
            first_even[r] = jnp.maximum(dot(patch, taps[r, :, 0:256]), 0.0).astype(BF16)
            first_odd[r + 1] = jnp.maximum(dot(patch, taps[r, :, 256:512]), 0.0).astype(BF16)

        def three_bins(rows):
            return jnp.concatenate(
                [
                    jnp.concatenate(
                        [first_odd[r, rows], first_even[r, rows], first_odd[r + 1, rows]], axis=1
                    )
                    for r in range(4)
                ],
                axis=0,
            )

        sums = dot(three_bins(slice(0, EVEN)), w2_even[...])
        sums_odd = dot(three_bins(slice(EVEN, ROWS)), w2_odd[...])
        second = []
        for r in range(4):
            here = sums[r * EVEN : (r + 1) * EVEN]
            later = pltpu.roll(here[:, 128:256], EVEN - 1, 0)[:FRAMES]
            total = here[:FRAMES, 0:128] * kept + later + sums_odd[r * FRAMES : (r + 1) * FRAMES]
            second.append(jnp.maximum(total + bias2, 0.0))
        for to in range(SIDE):
            mixed = second[to]
            for r in range(4):
                if r != to:
                    turned = pltpu.roll(second[r], (8 * (r - to)) % 128, 1)
                    mixed = jnp.where(lane_slot == r, turned, mixed)
            maps_out[to, g] = mixed.astype(BF16)
        for dx in (2, 1, 3):
            maps_copy(dx, g).start()
        for step, at in ((0, 0), (1, 4)):
            pl.when(g == at)(lambda step=step: w_step(step))
        return carry

    def maps_sent():
        def step(g, carry):
            for dx in range(1, SIDE):
                maps_copy(dx, g).wait_send()
            return carry

        lax.fori_loop(0, TILES, step, 0)

    drain.append(maps_sent)
    first_odd[4] = jnp.zeros((ROWS, 256), BF16)
    lax.fori_loop(0, TILES, convolve, 0)
    w_step(2)

    for g in range(TILES):
        maps_in[x, g] = maps_out[x, g]

    def maps_wait(g, carry):
        for dx in range(1, SIDE):
            maps_copy(dx, g).wait_recv()
        return carry

    lax.fori_loop(0, TILES, maps_wait, 0)
    for k in range(4):
        w_along_z(k).wait_recv()
    for k in (4, 5, 8, 9):
        w_along_y(k).wait_recv()

    mine = pl.ds(pl.multiple_of(phase * HALF, HALF), HALF)
    theirs = pl.ds(pl.multiple_of(other * HALF, HALF), HALF)

    def sib_copy(n):
        return remote(
            sib_out.at[n], sib_in.at[n], sib_send.at[n], sib_recv.at[n], {"phase": other}
        )

    def rs_copy(dx, n):
        return remote(
            rs_out.at[n, (x + dx) % SIDE],
            rs_in.at[dx - 1, n],
            rs_send.at[dx - 1, n],
            rs_recv.at[dx - 1, n],
            {"seq": row_peer(dx)},
        )

    def project(n):
        cols = pl.ds(pl.multiple_of(n * CUT, CUT), CUT)
        maps = jnp.concatenate(
            [
                jnp.concatenate([maps_in[s, g] for g in range(TILES)], axis=1)
                for s in range(SIDE)
            ],
            axis=0,
        )
        weights = w_all[:, :, cols].reshape(TILES * 128, CUT)
        part[n] = dot(maps, weights).reshape(SIDE, FRAMES, CUT)
        sib_out[n] = part[n, :, theirs, :].astype(BF16)
        sib_copy(n).start()

    def pass_on(n):
        sib_copy(n).wait_recv()
        both = part[n, :, mine, :] + sib_in[n].astype(F32)
        tot[n] = both
        rs_out[n] = both.astype(BF16)
        for dx in (2, 1, 3):
            rs_copy(dx, n).start()

    def project_step(n, carry):
        @pl.when(n < CUTS)
        def _():
            project(n)

        @pl.when(n >= 2)
        def _():
            pass_on(n - 2)

        return carry

    def sums_sent():
        def step(n, carry):
            sib_copy(n).wait_send()
            for dx in range(1, SIDE):
                rs_copy(dx, n).wait_send()
            return carry

        lax.fori_loop(0, CUTS, step, 0)

    drain.append(sums_sent)
    lax.fori_loop(0, CUTS + 2, project_step, 0)

    proj_bias = row_of(pb_ref)
    for n in range(CUTS):
        cols = slice(n * CUT, (n + 1) * CUT)
        for dx in range(1, SIDE):
            rs_copy(dx, n).wait_recv()
        total = tot[n, x]
        for dx in range(1, SIDE):
            total = total + rs_in[dx - 1, n].astype(F32)
        frames_mine[:, cols] = (total + proj_bias[:, cols]).astype(BF16)
    frames_copy = remote(
        frames_mine.at[:, pl.ds(pl.multiple_of(other * LOCAL, LOCAL), LOCAL)],
        frames_cols.at[mine, :],
        fr_send,
        fr_recv,
        {"phase": other},
    )
    frames_copy.start()
    drain.append(frames_copy.wait_send)
    numbers = frames_mine[...].astype(F32)
    average = jnp.mean(numbers, axis=1, keepdims=True)
    centered = numbers - average
    variance = jnp.mean(centered * centered, axis=1, keepdims=True)
    own_slot = pl.ds(pl.multiple_of(REACH * FRAMES + phase * HALF, HALF), HALF)
    normed[own_slot, :] = (centered * lax.rsqrt(variance + 1e-05) * row_of(gain_ref)).astype(BF16)

    def slot(d, k):
        return pl.ds(
            pl.multiple_of((REACH + d) * FRAMES + phase * HALF + k * QUARTER, QUARTER), QUARTER
        )

    def near_copy(d, k):
        step = 1 if d > 0 else -1
        source = normed.at[slot(d - step, k), :]
        target = normed.at[slot(d, k), :]
        sem = (NEAR.index(d), k)
        return remote(source, target, n_send.at[sem], n_recv.at[sem], {"seq": near_peer(-step)})

    def share_copy(d, k):
        rows = normed.at[slot(d, k), :]
        sem = (d + REACH, k)
        return remote(rows, rows, s_send.at[sem], s_recv.at[sem], {"phase": other})

    def near_sent():
        for k in range(2):
            for d in NEAR:
                near_copy(d, k).wait_send()
            for d in range(-REACH, REACH + 1):
                share_copy(d, k).wait_send()

    drain.append(near_sent)
    for k in range(2):
        for d in (-1, 1):
            near_copy(d, k).start()
        share_copy(0, k).start()
    frames_cols[mine, :] = frames_mine[:, pl.ds(pl.multiple_of(phase * LOCAL, LOCAL), LOCAL)]
    qkv_copy.wait()
    out_copy.wait()
    for k in range(2):
        share_copy(0, k).wait_recv()

    def keys_values(low, rows):
        block_rows = normed[low : low + rows, :]
        for n in range(3):
            cols = slice(n * CUT, (n + 1) * CUT)
            keys[low : low + rows, cols] = dot(block_rows, qkv_w[1, :, cols]).astype(BF16)
            values[low : low + rows, cols] = dot(block_rows, qkv_w[2, :, cols]).astype(BF16)

    own_low = REACH * FRAMES
    own_block = normed[own_low : own_low + FRAMES, :]
    for n in range(3):
        cols = slice(n * CUT, (n + 1) * CUT)
        made = dot(own_block, qkv_w[0, :, cols]).astype(BF16)
        query[:, cols] = made * jnp.asarray(1.0 / math.sqrt(HEAD), BF16)
    keys_values(own_low, FRAMES)
    for distance in (1, 2):
        for k in range(2):
            for d in (-distance, distance):
                near_copy(d, k).wait_recv()
                if distance == 1:
                    near_copy(2 * d, k).start()
                share_copy(d, k).start()
        for d in (-distance, distance):
            for k in range(2):
                share_copy(d, k).wait_recv()
            keys_values((REACH + d) * FRAMES, FRAMES)

    lane_low = lax.broadcasted_iota(jnp.int32, (FRAMES, 128), 1) < HEAD

    def attend(pair, carry):
        cols = pl.ds(pl.multiple_of(pair * 128, 128), 128)
        both = query[:, cols]
        zero = jnp.zeros_like(both)
        stacked = jnp.concatenate(
            [jnp.where(lane_low, both, zero), jnp.where(lane_low, zero, both)], axis=0
        )
        scores = lax.dot_general(
            stacked, keys[:, cols], (((1,), (1,)), ((), ())), preferred_element_type=F32
        )
        mask = bias_mask[...]
        scores = scores + jnp.concatenate([mask, mask], axis=0)
        highest = jnp.max(scores, axis=1, keepdims=True)
        weight = jnp.exp(scores - highest)
        denominator = jnp.sum(weight, axis=1, keepdims=True)
        mixed = dot(weight.astype(BF16), values[:, cols]) / denominator
        context[:, cols] = jnp.where(lane_low, mixed[:FRAMES], mixed[FRAMES:]).astype(BF16)
        return carry

    lax.fori_loop(0, LOCAL // 128, attend, 0)

    def br_copy(n):
        return remote(br_out.at[n], br_in.at[n], br_send.at[n], br_recv.at[n], {"phase": other})

    for n in range(3):
        cols = pl.ds(pl.multiple_of(other * LOCAL + n * CUT, CUT), CUT)
        br_out[n] = dot(context[...], out_w[:, cols]).astype(BF16)
        br_copy(n).start()
        drain.append(br_copy(n).wait_send)
    frames_copy.wait_recv()
    for n in range(3):
        cols = pl.ds(pl.multiple_of(phase * LOCAL + n * CUT, CUT), CUT)
        here = slice(n * CUT, (n + 1) * CUT)
        total = frames_cols[:, here].astype(F32) + dot(context[...], out_w[:, cols])
        br_copy(n).wait_recv()
        out_ref[:, here] = (total + br_in[n].astype(F32)).astype(BF16)

    for wait in drain:
        wait()


def local(
    features,
    lengths,
    conv1_weight,
    conv1_bias,
    conv2_weight,
    conv2_bias,
    proj_weight,
    proj_bias,
    norm_gain,
    qkv_weight,
    out_weight,
):
    vmem = pl.BlockSpec(memory_space=pltpu.VMEM)
    smem = pl.BlockSpec(memory_space=pltpu.SMEM)
    hbm = pl.BlockSpec(memory_space=pl.ANY)
    dma = pltpu.SemaphoreType.DMA
    scratch = [
        pltpu.VMEM((4 * FRAMES, 128), BF16),
        pltpu.VMEM((3, 3, 256), F32),
        pltpu.VMEM((2, 128), F32),
        pltpu.VMEM((1, 128), F32),
        pltpu.VMEM((256, WIDTH), BF16),
        pltpu.VMEM((WIDTH // 128, 128), F32),
        pltpu.VMEM((WIDTH // 128, 128), F32),
        pltpu.VMEM((16, 128), BF16),
        pltpu.VMEM((PADDED, 128), F32),
        pltpu.VMEM((384, BINS * 32), BF16),
        pltpu.VMEM((32, 512), F32),
        pltpu.VMEM((4, 128, 512), BF16),
        pltpu.VMEM((TILES, ROWS, 128), BF16),
        pltpu.VMEM((768, 256), BF16),
        pltpu.VMEM((768, 128), BF16),
        pltpu.VMEM((4, ROWS, 256), BF16),
        pltpu.VMEM((5, ROWS, 256), BF16),
        pltpu.VMEM((TILES, 128, WIDTH), BF16),
        pltpu.VMEM((SIDE, TILES, FRAMES, 128), BF16),
        pltpu.VMEM((SIDE, TILES, FRAMES, 128), BF16),
        pltpu.VMEM((CUTS, SIDE, FRAMES, CUT), F32),
        pltpu.VMEM((CUTS, SIDE, HALF, CUT), BF16),
        pltpu.VMEM((CUTS, SIDE, HALF, CUT), BF16),
        pltpu.VMEM((CUTS, SIDE, HALF, CUT), F32),
        pltpu.VMEM((CUTS, SIDE, HALF, CUT), BF16),
        pltpu.VMEM((SIDE - 1, CUTS, HALF, CUT), BF16),
        pltpu.VMEM((HALF, WIDTH), BF16),
        pltpu.VMEM((FRAMES, LOCAL), BF16),
        pltpu.VMEM((SPAN, WIDTH), BF16),
        pltpu.VMEM((3, WIDTH, LOCAL), BF16),
        pltpu.VMEM((LOCAL, WIDTH), BF16),
        pltpu.VMEM((FRAMES, LOCAL), BF16),
        pltpu.VMEM((SPAN, LOCAL), BF16),
        pltpu.VMEM((SPAN, LOCAL), BF16),
        pltpu.VMEM((FRAMES, SPAN), F32),
        pltpu.VMEM((FRAMES, LOCAL), BF16),
        pltpu.VMEM((3, FRAMES, CUT), BF16),
        pltpu.VMEM((3, FRAMES, CUT), BF16),
        dma((7,)),
        dma((9,)),
        dma,
        dma,
        dma,
        dma,
        dma((10,)),
        dma((10,)),
        dma((4,)),
        dma((4,)),
        dma((3, TILES)),
        dma((3, TILES)),
        dma((CUTS,)),
        dma((CUTS,)),
        dma((3, CUTS)),
        dma((3, CUTS)),
        dma,
        dma,
        dma((4, 2)),
        dma((4, 2)),
        dma((5, 2)),
        dma((5, 2)),
        dma((3,)),
        dma((3,)),
    ]
    encoded = pl.pallas_call(
        body,
        out_shape=jax.ShapeDtypeStruct((FRAMES, LOCAL), BF16),
        in_specs=[smem] + [hbm] * 10,
        out_specs=vmem,
        scratch_shapes=scratch,
        compiler_params=pltpu.CompilerParams(
            collective_id=0, has_side_effects=True, vmem_limit_bytes=60 * 1024 * 1024
        ),
    )(
        lengths,
        features[0],
        conv1_weight,
        conv1_bias.reshape(2, 128),
        conv2_weight,
        conv2_bias[None],
        proj_weight,
        proj_bias.reshape(WIDTH // 128, 128),
        norm_gain.reshape(WIDTH // 128, 128),
        qkv_weight.transpose(1, 0, 2),
        out_weight,
    )
    return encoded[None]


def solution(mesh):
    in_specs = (
        P("batch", "seq", None),
        P("batch", None),
        P(),
        P(),
        P(None, None, None, "phase"),
        P("phase"),
        P(("phase", "seq"), None),
        P(),
        P(),
        P(None, None, "phase"),
        P("phase", None),
    )
    out_specs = P("batch", "seq", "phase")
    return jax.shard_map(local, mesh=mesh, in_specs=in_specs, out_specs=out_specs, check_vma=False)
```

```python
import math

import jax
import jax.numpy as jnp
from jax import lax
from jax.experimental import pallas as pl
from jax.experimental.pallas import tpu as pltpu
from jax.sharding import PartitionSpec as P

MESH = pl.DeviceIdType.MESH
BF16 = jnp.bfloat16
F32 = jnp.float32

SIDE = 4
BLOCKS = SIDE * SIDE
FRAMES = 128
HALF = 64
QUARTER = 32
BINS = 32
UTTS = 12
WIDTH = 1536
LOCAL = 768
HEAD = 64
EVEN = 144
ROWS = EVEN + FRAMES
PADDED = 584
TILES = 8
CUT = 256
CUTS = WIDTH // CUT
REACH = 2
SPAN = (2 * REACH + 1) * FRAMES
NEAR = (-2, -1, 1, 2)


def dot(a, b):
    return jnp.dot(a, b, preferred_element_type=F32)


def body(
    lengths_ref,
    feat_hbm,
    w1_hbm,
    b1_hbm,
    w2_ref,
    b2_hbm,
    wp_hbm,
    pb_hbm,
    gain_hbm,
    qkv_ref,
    wo_ref,
    out_ref,
    feat_ref,
    w1_ref,
    b1_ref,
    b2_ref,
    wp_ref,
    pb_ref,
    gain_ref,
    halo,
    padded,
    picker,
    base,
    taps,
    patches,
    w2_even,
    w2_odd,
    first_even,
    first_odd,
    w_all,
    maps_out,
    maps_in,
    part,
    sib_out,
    sib_in,
    tot,
    rs_out,
    rs_in,
    relay_in,
    relay_out,
    frames_mine,
    frames_cols,
    normed,
    qkv_w,
    out_w,
    query,
    keys,
    values,
    bias_mask,
    context,
    br_out,
    br_in,
    in_sem,
    w2_sem,
    qkv_sem,
    out_sem,
    halo_send,
    halo_recv,
    wy_send,
    wy_recv,
    wz_send,
    wz_recv,
    m_send,
    m_recv,
    sib_send,
    sib_recv,
    rs_send,
    rs_recv,
    fr_send,
    fr_recv,
    n_send,
    n_recv,
    s_send,
    s_recv,
    br_send,
    br_recv,
):
    phase = lax.axis_index("phase")
    block = lax.axis_index("seq")
    x = block % SIDE
    y = block // SIDE
    plane = lax.axis_index("batch")
    partner = plane + 1 - 2 * (plane % 2)
    other = 1 - phase

    def row_of(ref):
        return jnp.concatenate([ref[k : k + 1, :] for k in range(WIDTH // 128)], axis=1)

    def row_peer(dx):
        return y * SIDE + (x + dx + SIDE) % SIDE

    def column_peer(dy):
        return ((y + dy + SIDE) % SIDE) * SIDE + x

    def near_peer(d):
        return (block + d + BLOCKS) % BLOCKS

    def remote(src, dst, send, recv, target):
        return pltpu.make_async_remote_copy(
            src_ref=src,
            dst_ref=dst,
            send_sem=send,
            recv_sem=recv,
            device_id=target,
            device_id_type=MESH,
        )

    inputs = [
        pltpu.make_async_copy(source, target, in_sem.at[k])
        for k, (source, target) in enumerate(
            (
                (wp_hbm, wp_ref),
                (feat_hbm, feat_ref),
                (w1_hbm, w1_ref),
                (b1_hbm, b1_ref),
                (b2_hbm, b2_ref),
                (pb_hbm, pb_ref),
                (gain_hbm, gain_ref),
            )
        )
    ]
    for copy in inputs:
        copy.start()
    local_w2 = []
    for b in range(3):
        rows = pl.ds(b * 256, 256)
        local_w2.append(
            pltpu.make_async_copy(w2_ref.at[0, b], w2_even.at[rows, pl.ds(0, 128)], w2_sem.at[b])
        )
        local_w2.append(
            pltpu.make_async_copy(
                w2_ref.at[2, b], w2_even.at[rows, pl.ds(128, 128)], w2_sem.at[3 + b]
            )
        )
        local_w2.append(pltpu.make_async_copy(w2_ref.at[1, b], w2_odd.at[rows], w2_sem.at[6 + b]))
    for copy in local_w2:
        copy.start()
    qkv_copy = pltpu.make_async_copy(qkv_ref, qkv_w, qkv_sem)
    out_copy = pltpu.make_async_copy(wo_ref, out_w, out_sem)
    qkv_copy.start()
    out_copy.start()

    barrier = pltpu.get_barrier_semaphore()
    peers = [{"phase": other}]
    peers += [{"seq": row_peer(dx)} for dx in range(1, SIDE)]
    peers += [{"seq": column_peer(dy)} for dy in (1, 3)]
    peers += [{"batch": partner}]
    peers += [{"seq": near_peer(d)} for d in (1, -1)]
    for peer in peers:
        pl.semaphore_signal(barrier, inc=1, device_id=peer, device_id_type=MESH)

    out_row = lax.broadcasted_iota(jnp.int32, (256, 256), 0)
    in_row = lax.broadcasted_iota(jnp.int32, (256, 256), 1)
    reorder = jnp.where(in_row == (out_row & 7) * BINS + (out_row >> 3), 1.0, 0.0).astype(BF16)
    own_rows = pl.ds(pl.multiple_of(y * 32, 32), 32)
    inputs[0].wait()
    for n in range(CUTS):
        cols = slice(n * CUT, (n + 1) * CUT)
        moved = dot(reorder, wp_ref[:, cols]).astype(BF16)
        for g in range(TILES):
            w_all[g, own_rows, cols] = moved[g * 32 : (g + 1) * 32]

    inputs[1].wait()
    pl.semaphore_wait(barrier, len(peers))

    halo_copy = remote(
        feat_ref.at[pl.ds(496, 16)], halo, halo_send, halo_recv, {"seq": near_peer(1)}
    )
    halo_copy.start()
    drain = [halo_copy.wait_send]
    own_groups = 2 * (plane % 2)
    along_y = [
        (-1, own_groups, 2, -1),
        (1, own_groups, 2, 1),
        (-1, 4, 2, -1),
        (1, 6, 2, 1),
        (-1, 6, 2, -1),
        (1, 4, 2, 1),
        (2, own_groups, 1, -1),
        (2, own_groups + 1, 1, 1),
        (2, 4, 2, -1),
        (2, 6, 2, 1),
    ]
    along_z = [
        (-1, own_groups, 2),
        (1, own_groups, 2),
        (2, own_groups, 1),
        (2, own_groups + 1, 1),
    ]

    def w_piece(dy, low, groups):
        rows = pl.ds(pl.multiple_of(((y + dy + SIDE) % SIDE) * 32, 32), 32)
        return w_all.at[pl.ds(low, groups), rows, :]

    def w_along_y(k):
        dy, low, groups, side = along_y[k]
        piece = w_piece(dy - side, low, groups)
        return remote(piece, piece, wy_send.at[k], wy_recv.at[k], {"seq": column_peer(-side)})

    def w_along_z(k):
        piece = w_piece(*along_z[k])
        return remote(piece, piece, wz_send.at[k], wz_recv.at[k], {"batch": partner})

    def w_sent():
        for k in range(10):
            w_along_y(k).wait_send()
        for k in range(4):
            w_along_z(k).wait_send()

    drain.append(w_sent)
    for k in range(4):
        w_along_y(k).start()

    def w_step(step):
        if step == 0:
            for k in (0, 1):
                w_along_y(k).wait_recv()
                w_along_y(6 + k).start()
                w_along_z(k).start()
            for k in (4, 5):
                w_along_y(k).start()
        if step == 1:
            for k in (2, 3):
                w_along_y(k).wait_recv()
                w_along_y(6 + k).start()
        if step == 2:
            for k in (6, 7):
                w_along_y(k).wait_recv()
                w_along_z(k - 4).start()

    offsets = []
    running = jnp.int32(0)
    for i in range(UTTS):
        offsets.append(running)
        running = running + lengths_ref[0, i]
    place = lax.broadcasted_iota(jnp.int32, (FRAMES, 128), 0) + block * FRAMES
    starts = place == offsets[0]
    seg_query = jnp.where(place >= offsets[0], 1, 0)
    for off in offsets[1:]:
        starts = starts | (place == off)
        seg_query = seg_query + jnp.where(place >= off, 1, 0)
    kept = jnp.where(starts, 0.0, 1.0)
    key_place = lax.broadcasted_iota(jnp.int32, (8, SPAN), 1) + (block - REACH) * FRAMES
    seg_key = jnp.where(key_place >= offsets[0], 1, 0)
    for off in offsets[1:]:
        seg_key = seg_key + jnp.where(key_place >= off, 1, 0)
    seg_key = jnp.where((key_place >= 0) & (key_place < BLOCKS * FRAMES), seg_key, 0)
    for j in range(SPAN // 128):
        cols = slice(j * 128, (j + 1) * 128)
        bias_mask[:, cols] = jnp.where(seg_query == seg_key[0:1, cols], 0.0, -1e30)

    for copy in inputs[2:]:
        copy.wait()
    base[...] = jnp.zeros_like(base)

    def two_pieces(value):
        high = value.astype(BF16).astype(F32)
        return high, value - high

    for a in range(3):
        pair = two_pieces(w1_ref[a])
        for b in range(3):
            for shift in range(2):
                for k in range(2):
                    row = 15 * k + 5 * a + 2 * shift + b
                    base[row : row + 1, shift * 256 : (shift + 1) * 256] = pair[k][b : b + 1, :]
    pair = two_pieces(jnp.concatenate([b1_ref[0:1, :], b1_ref[1:2, :]], axis=1))
    for k in range(2):
        for shift in range(2):
            base[30 + k : 31 + k, shift * 256 : (shift + 1) * 256] = pair[k]
    taps[...] = jnp.zeros_like(taps)
    for r in range(4):
        taps[r, 32 * r : 32 * r + 32, :] = base[...].astype(BF16)

    lane = lax.broadcasted_iota(jnp.int32, (1, BINS * 32), 1)
    low = lane & 31
    tap = jnp.where(low >= 15, low - 15, low)
    tap_time = jnp.where(tap >= 5, 1, 0) + jnp.where(tap >= 10, 1, 0)
    tap_bin = (lane >> 5) * 4 + (tap - 5 * tap_time) - 1
    wanted = jnp.where((low < 30) & (tap_bin >= 0), tap_time * 128 + tap_bin, -1)
    constant = jnp.where(low >= 30, 1.0, 0.0)
    for a in range(3):
        bins_in = lax.broadcasted_iota(jnp.int32, (128, BINS * 32), 0) + a * 128
        picker[a * 128 : (a + 1) * 128, :] = jnp.where(bins_in == wanted, 1.0, 0.0).astype(BF16)

    padded[8:520, :] = feat_ref[...].astype(F32)
    padded[520:PADDED, :] = jnp.zeros((PADDED - 520, 128), F32)
    halo_copy.wait_recv()
    first = jnp.where(block > 0, 1.0, 0.0)
    padded[0:8, :] = halo[...].astype(F32)[8:16] * first
    even = [padded[pl.ds(5 + a, EVEN, stride=4), :] for a in range(3)]
    odd = [padded[pl.ds(7 + a, FRAMES, stride=4), :] for a in range(3)]
    odd[0] = odd[0] * kept
    gathered = jnp.concatenate(
        [jnp.concatenate(even, axis=1), jnp.concatenate(odd, axis=1)], axis=0
    ).astype(BF16)
    for k in range(4):
        cols = slice(k * 256, (k + 1) * 256)
        made = (dot(gathered, picker[:, cols]) + constant[:, cols]).astype(BF16)
        patches[2 * k] = made[:, 0:128]
        patches[2 * k + 1] = made[:, 128:256]

    for copy in local_w2:
        copy.wait()

    lane_slot = (lax.broadcasted_iota(jnp.int32, (FRAMES, 128), 1) >> 3) & 3
    bias2 = b2_ref[...]

    def maps_copy(dx, g):
        return remote(
            maps_out.at[(x + dx) % SIDE, g],
            maps_in.at[x, g],
            m_send.at[dx - 1, g],
            m_recv.at[dx - 1, g],
            {"seq": row_peer(dx)},
        )

    def convolve(g, carry):
        patch = patches[g]
        first_odd[0] = first_odd[4]
        for r in range(4):
            first_even[r] = jnp.maximum(dot(patch, taps[r, :, 0:256]), 0.0).astype(BF16)
            first_odd[r + 1] = jnp.maximum(dot(patch, taps[r, :, 256:512]), 0.0).astype(BF16)

        def three_bins(rows):
            return jnp.concatenate(
                [
                    jnp.concatenate(
                        [first_odd[r, rows], first_even[r, rows], first_odd[r + 1, rows]], axis=1
                    )
                    for r in range(4)
                ],
                axis=0,
            )

        sums = dot(three_bins(slice(0, EVEN)), w2_even[...])
        sums_odd = dot(three_bins(slice(EVEN, ROWS)), w2_odd[...])
        second = []
        for r in range(4):
            here = sums[r * EVEN : (r + 1) * EVEN]
            later = pltpu.roll(here[:, 128:256], EVEN - 1, 0)[:FRAMES]
            total = here[:FRAMES, 0:128] * kept + later + sums_odd[r * FRAMES : (r + 1) * FRAMES]
            second.append(jnp.maximum(total + bias2, 0.0))
        for to in range(SIDE):
            mixed = second[to]
            for r in range(4):
                if r != to:
                    turned = pltpu.roll(second[r], (8 * (r - to)) % 128, 1)
                    mixed = jnp.where(lane_slot == r, turned, mixed)
            maps_out[to, g] = mixed.astype(BF16)
        for dx in (2, 1, 3):
            maps_copy(dx, g).start()
        for step, at in ((0, 0), (1, 4)):
            pl.when(g == at)(lambda step=step: w_step(step))
        return carry

    def maps_sent():
        def step(g, carry):
            for dx in range(1, SIDE):
                maps_copy(dx, g).wait_send()
            return carry

        lax.fori_loop(0, TILES, step, 0)

    drain.append(maps_sent)
    first_odd[4] = jnp.zeros((ROWS, 256), BF16)
    lax.fori_loop(0, TILES, convolve, 0)
    w_step(2)

    for g in range(TILES):
        maps_in[x, g] = maps_out[x, g]

    def maps_wait(g, carry):
        for dx in range(1, SIDE):
            maps_copy(dx, g).wait_recv()
        return carry

    lax.fori_loop(0, TILES, maps_wait, 0)
    for k in range(4):
        w_along_z(k).wait_recv()
    for k in (4, 5, 8, 9):
        w_along_y(k).wait_recv()

    mine = pl.ds(pl.multiple_of(phase * HALF, HALF), HALF)
    theirs = pl.ds(pl.multiple_of(other * HALF, HALF), HALF)

    def sib_copy(n):
        return remote(
            sib_out.at[n], sib_in.at[n], sib_send.at[n], sib_recv.at[n], {"phase": other}
        )

    def way(n):
        return 1 - 2 * (n % 2)

    def through_copy(n):
        return remote(
            rs_out.at[n, (x + 2) % SIDE],
            relay_in.at[n],
            rs_send.at[2, n],
            rs_recv.at[2, n],
            {"seq": row_peer(way(n))},
        )

    def back_copy(n):
        return remote(
            rs_out.at[n, (x - way(n) + SIDE) % SIDE],
            rs_in.at[0, n],
            rs_send.at[0, n],
            rs_recv.at[0, n],
            {"seq": row_peer(-way(n))},
        )

    def joint_copy(n):
        return remote(
            relay_out.at[n],
            rs_in.at[1, n],
            rs_send.at[1, n],
            rs_recv.at[1, n],
            {"seq": row_peer(way(n))},
        )

    def relay(n):
        through_copy(n).wait_recv()
        added = tot[n, (x + way(n) + SIDE) % SIDE] + relay_in[n].astype(F32)
        relay_out[n] = added.astype(BF16)
        joint_copy(n).start()

    def project(n):
        cols = pl.ds(pl.multiple_of(n * CUT, CUT), CUT)
        maps = jnp.concatenate(
            [
                jnp.concatenate([maps_in[s, g] for g in range(TILES)], axis=1)
                for s in range(SIDE)
            ],
            axis=0,
        )
        weights = w_all[:, :, cols].reshape(TILES * 128, CUT)
        part[n] = dot(maps, weights).reshape(SIDE, FRAMES, CUT)
        sib_out[n] = part[n, :, theirs, :].astype(BF16)
        sib_copy(n).start()

    def pass_on(n):
        sib_copy(n).wait_recv()
        both = part[n, :, mine, :] + sib_in[n].astype(F32)
        tot[n] = both
        rs_out[n] = both.astype(BF16)
        through_copy(n).start()
        back_copy(n).start()

    def project_step(n, carry):
        @pl.when(n < CUTS)
        def _():
            project(n)

        @pl.when((n >= 2) & (n < CUTS + 2))
        def _():
            pass_on(n - 2)

        @pl.when(n >= 5)
        def _():
            relay(n - 5)

        return carry

    def sums_sent():
        def step(n, carry):
            sib_copy(n).wait_send()
            for copy in (through_copy, back_copy, joint_copy):
                copy(n).wait_send()
            return carry

        lax.fori_loop(0, CUTS, step, 0)

    drain.append(sums_sent)
    lax.fori_loop(0, CUTS + 5, project_step, 0)

    proj_bias = row_of(pb_ref)
    for n in range(CUTS):
        cols = slice(n * CUT, (n + 1) * CUT)
        back_copy(n).wait_recv()
        joint_copy(n).wait_recv()
        total = tot[n, x] + rs_in[0, n].astype(F32) + rs_in[1, n].astype(F32)
        frames_mine[:, cols] = (total + proj_bias[:, cols]).astype(BF16)
    frames_copy = remote(
        frames_mine.at[:, pl.ds(pl.multiple_of(other * LOCAL, LOCAL), LOCAL)],
        frames_cols.at[mine, :],
        fr_send,
        fr_recv,
        {"phase": other},
    )
    frames_copy.start()
    drain.append(frames_copy.wait_send)
    numbers = frames_mine[...].astype(F32)
    average = jnp.mean(numbers, axis=1, keepdims=True)
    centered = numbers - average
    variance = jnp.mean(centered * centered, axis=1, keepdims=True)
    own_slot = pl.ds(pl.multiple_of(REACH * FRAMES + phase * HALF, HALF), HALF)
    normed[own_slot, :] = (centered * lax.rsqrt(variance + 1e-05) * row_of(gain_ref)).astype(BF16)

    def slot(d, k):
        return pl.ds(
            pl.multiple_of((REACH + d) * FRAMES + phase * HALF + k * QUARTER, QUARTER), QUARTER
        )

    def near_copy(d, k):
        step = 1 if d > 0 else -1
        source = normed.at[slot(d - step, k), :]
        target = normed.at[slot(d, k), :]
        sem = (NEAR.index(d), k)
        return remote(source, target, n_send.at[sem], n_recv.at[sem], {"seq": near_peer(-step)})

    def share_copy(d, k):
        rows = normed.at[slot(d, k), :]
        sem = (d + REACH, k)
        return remote(rows, rows, s_send.at[sem], s_recv.at[sem], {"phase": other})

    def near_sent():
        for k in range(2):
            for d in NEAR:
                near_copy(d, k).wait_send()
            for d in range(-REACH, REACH + 1):
                share_copy(d, k).wait_send()

    drain.append(near_sent)
    for k in range(2):
        for d in (-1, 1):
            near_copy(d, k).start()
        share_copy(0, k).start()
    frames_cols[mine, :] = frames_mine[:, pl.ds(pl.multiple_of(phase * LOCAL, LOCAL), LOCAL)]
    qkv_copy.wait()
    out_copy.wait()
    for k in range(2):
        share_copy(0, k).wait_recv()

    def keys_values(low, rows):
        block_rows = normed[low : low + rows, :]
        for n in range(3):
            cols = slice(n * CUT, (n + 1) * CUT)
            keys[low : low + rows, cols] = dot(block_rows, qkv_w[1, :, cols]).astype(BF16)
            values[low : low + rows, cols] = dot(block_rows, qkv_w[2, :, cols]).astype(BF16)

    own_low = REACH * FRAMES
    own_block = normed[own_low : own_low + FRAMES, :]
    for n in range(3):
        cols = slice(n * CUT, (n + 1) * CUT)
        made = dot(own_block, qkv_w[0, :, cols]).astype(BF16)
        query[:, cols] = made * jnp.asarray(1.0 / math.sqrt(HEAD), BF16)
    keys_values(own_low, FRAMES)
    for distance in (1, 2):
        for k in range(2):
            for d in (-distance, distance):
                near_copy(d, k).wait_recv()
                if distance == 1:
                    near_copy(2 * d, k).start()
                share_copy(d, k).start()
        for d in (-distance, distance):
            for k in range(2):
                share_copy(d, k).wait_recv()
            keys_values((REACH + d) * FRAMES, FRAMES)

    lane_low = lax.broadcasted_iota(jnp.int32, (FRAMES, 128), 1) < HEAD

    def attend(pair, carry):
        cols = pl.ds(pl.multiple_of(pair * 128, 128), 128)
        both = query[:, cols]
        zero = jnp.zeros_like(both)
        stacked = jnp.concatenate(
            [jnp.where(lane_low, both, zero), jnp.where(lane_low, zero, both)], axis=0
        )
        scores = lax.dot_general(
            stacked, keys[:, cols], (((1,), (1,)), ((), ())), preferred_element_type=F32
        )
        mask = bias_mask[...]
        scores = scores + jnp.concatenate([mask, mask], axis=0)
        highest = jnp.max(scores, axis=1, keepdims=True)
        weight = jnp.exp(scores - highest)
        denominator = jnp.sum(weight, axis=1, keepdims=True)
        mixed = dot(weight.astype(BF16), values[:, cols]) / denominator
        context[:, cols] = jnp.where(lane_low, mixed[:FRAMES], mixed[FRAMES:]).astype(BF16)
        return carry

    lax.fori_loop(0, LOCAL // 128, attend, 0)

    def br_copy(n):
        return remote(br_out.at[n], br_in.at[n], br_send.at[n], br_recv.at[n], {"phase": other})

    for n in range(3):
        cols = pl.ds(pl.multiple_of(other * LOCAL + n * CUT, CUT), CUT)
        br_out[n] = dot(context[...], out_w[:, cols]).astype(BF16)
        br_copy(n).start()
        drain.append(br_copy(n).wait_send)
    frames_copy.wait_recv()
    for n in range(3):
        cols = pl.ds(pl.multiple_of(phase * LOCAL + n * CUT, CUT), CUT)
        here = slice(n * CUT, (n + 1) * CUT)
        total = frames_cols[:, here].astype(F32) + dot(context[...], out_w[:, cols])
        br_copy(n).wait_recv()
        out_ref[:, here] = (total + br_in[n].astype(F32)).astype(BF16)

    for wait in drain:
        wait()


def local(
    features,
    lengths,
    conv1_weight,
    conv1_bias,
    conv2_weight,
    conv2_bias,
    proj_weight,
    proj_bias,
    norm_gain,
    qkv_weight,
    out_weight,
):
    vmem = pl.BlockSpec(memory_space=pltpu.VMEM)
    smem = pl.BlockSpec(memory_space=pltpu.SMEM)
    hbm = pl.BlockSpec(memory_space=pl.ANY)
    dma = pltpu.SemaphoreType.DMA
    scratch = [
        pltpu.VMEM((4 * FRAMES, 128), BF16),
        pltpu.VMEM((3, 3, 256), F32),
        pltpu.VMEM((2, 128), F32),
        pltpu.VMEM((1, 128), F32),
        pltpu.VMEM((256, WIDTH), BF16),
        pltpu.VMEM((WIDTH // 128, 128), F32),
        pltpu.VMEM((WIDTH // 128, 128), F32),
        pltpu.VMEM((16, 128), BF16),
        pltpu.VMEM((PADDED, 128), F32),
        pltpu.VMEM((384, BINS * 32), BF16),
        pltpu.VMEM((32, 512), F32),
        pltpu.VMEM((4, 128, 512), BF16),
        pltpu.VMEM((TILES, ROWS, 128), BF16),
        pltpu.VMEM((768, 256), BF16),
        pltpu.VMEM((768, 128), BF16),
        pltpu.VMEM((4, ROWS, 256), BF16),
        pltpu.VMEM((5, ROWS, 256), BF16),
        pltpu.VMEM((TILES, 128, WIDTH), BF16),
        pltpu.VMEM((SIDE, TILES, FRAMES, 128), BF16),
        pltpu.VMEM((SIDE, TILES, FRAMES, 128), BF16),
        pltpu.VMEM((CUTS, SIDE, FRAMES, CUT), F32),
        pltpu.VMEM((CUTS, SIDE, HALF, CUT), BF16),
        pltpu.VMEM((CUTS, SIDE, HALF, CUT), BF16),
        pltpu.VMEM((CUTS, SIDE, HALF, CUT), F32),
        pltpu.VMEM((CUTS, SIDE, HALF, CUT), BF16),
        pltpu.VMEM((2, CUTS, HALF, CUT), BF16),
        pltpu.VMEM((CUTS, HALF, CUT), BF16),
        pltpu.VMEM((CUTS, HALF, CUT), BF16),
        pltpu.VMEM((HALF, WIDTH), BF16),
        pltpu.VMEM((FRAMES, LOCAL), BF16),
        pltpu.VMEM((SPAN, WIDTH), BF16),
        pltpu.VMEM((3, WIDTH, LOCAL), BF16),
        pltpu.VMEM((LOCAL, WIDTH), BF16),
        pltpu.VMEM((FRAMES, LOCAL), BF16),
        pltpu.VMEM((SPAN, LOCAL), BF16),
        pltpu.VMEM((SPAN, LOCAL), BF16),
        pltpu.VMEM((FRAMES, SPAN), F32),
        pltpu.VMEM((FRAMES, LOCAL), BF16),
        pltpu.VMEM((3, FRAMES, CUT), BF16),
        pltpu.VMEM((3, FRAMES, CUT), BF16),
        dma((7,)),
        dma((9,)),
        dma,
        dma,
        dma,
        dma,
        dma((10,)),
        dma((10,)),
        dma((4,)),
        dma((4,)),
        dma((3, TILES)),
        dma((3, TILES)),
        dma((CUTS,)),
        dma((CUTS,)),
        dma((3, CUTS)),
        dma((3, CUTS)),
        dma,
        dma,
        dma((4, 2)),
        dma((4, 2)),
        dma((5, 2)),
        dma((5, 2)),
        dma((3,)),
        dma((3,)),
    ]
    encoded = pl.pallas_call(
        body,
        out_shape=jax.ShapeDtypeStruct((FRAMES, LOCAL), BF16),
        in_specs=[smem] + [hbm] * 10,
        out_specs=vmem,
        scratch_shapes=scratch,
        compiler_params=pltpu.CompilerParams(
            collective_id=0, has_side_effects=True, vmem_limit_bytes=60 * 1024 * 1024
        ),
    )(
        lengths,
        features[0],
        conv1_weight,
        conv1_bias.reshape(2, 128),
        conv2_weight,
        conv2_bias[None],
        proj_weight,
        proj_bias.reshape(WIDTH // 128, 128),
        norm_gain.reshape(WIDTH // 128, 128),
        qkv_weight.transpose(1, 0, 2),
        out_weight,
    )
    return encoded[None]


def solution(mesh):
    in_specs = (
        P("batch", "seq", None),
        P("batch", None),
        P(),
        P(),
        P(None, None, None, "phase"),
        P("phase"),
        P(("phase", "seq"), None),
        P(),
        P(),
        P(None, None, "phase"),
        P("phase", None),
    )
    out_specs = P("batch", "seq", "phase")
    return jax.shard_map(local, mesh=mesh, in_specs=in_specs, out_specs=out_specs, check_vma=False)
```
